128 devices in a mesh: row: 16 (over y, x), col: 8 (over z, core).
Axes of the slice: x: 4, y: 4, z: 4, core: 2. Of those that a mesh axis runs over, the one named last changes fastest.
Arguments:
- new_rows: float32 [32768, 2048], P('row', 'col'), may hold values from -6 to 6
- old_rows: float32 [32768, 2048], P('row', 'col'), may hold values from -6 to 6
- row_ids: int32 [32768], P('row'), may hold values from 0 to 3999999
- owner: int32 [32768, 1], P('row'), may hold values from 0 to 127; in each aligned block of 256 rows (0 to 255, 256 to 511, ...) at most 4 rows name the same one
Outputs:
- published: bfloat16 [65536, 2048], P(('row', 'col'))
- row_scale: bfloat16 [65536], P(('row', 'col'))
- published_ids: int32 [65536], P(('row', 'col'))
The draws below stay inside these ranges and needn't reach their ends.
Inputs may be any that keep to these rules, and one draw needn't show every extreme that they name: Within one aligned block of 256 rows no owner is named more than 4 times, and in some block some owner is named exactly 4 times.
All inputs are finite; a program needn't handle non-finite values. Where the reference program divides by a largest or mean magnitude, that divisor is 1e-20 or more.
Results may differ from the reference program's by a relative error of at most 0.005.
Values may be sent and summed in bfloat16 or wider, within the bound.
A program may use at most 64 MiB of HBM per device.

```python
import math
import jax
import jax.numpy as jnp
import numpy as np
from jax import lax

D = 2048
TABLE = 4000000
ROWS_DEV = 2048
ROWS = 32768
BLK = 256
CAP = 4
N_ROW = 16
N_COL = 8
DEVICES = 128


def touch_ends(entries, own_key, least, top_value):
    index_at = [jax.random.randint(jax.random.fold_in(own_key, axis), (), 0, length) for axis, length in enumerate(entries.shape)]
    widest = entries.shape.index(max(entries.shape))
    neighbour = index_at[:widest] + [(index_at[widest] + 1) % entries.shape[widest]] + index_at[widest + 1:]
    return entries.at[tuple(index_at)].set(least).at[tuple(neighbour)].set(top_value)


def steps_of(key, dims, cuts, least, largest):
    def one(dim, parts):
        steps = jax.random.uniform(jax.random.fold_in(jax.random.fold_in(key, 6), dim), (parts,), jnp.float32, least / len(cuts), largest / len(cuts))
        return jnp.repeat(jnp.exp(steps), dims[dim] // parts).reshape((-1,) + (1,) * (len(dims) - dim - 1))

    factor_of = one(*cuts[0])
    for cut in cuts[1:]:
        factor_of = factor_of * one(*cut)
    return factor_of


def routed_block(own_key, own, number, rows, amount, top, most, skew):
    ranking = jax.random.permutation(own_key, amount)
    crowded, ordinary = load_shares(amount, rows * top, most, skew, True), load_shares(amount, rows * top, most, skew, False)
    places = jnp.arange(amount)

    def named(tallies, turn):
        used = int((tallies > 0).sum())
        fixed = max(1, used // 4)
        moved = fixed + (places - fixed + turn * (used - fixed)) % max(1, amount - fixed)
        return jnp.zeros((amount,), jnp.int32).at[ranking[jnp.where(places < fixed, places, moved)]].set(jnp.asarray(tallies, jnp.int32))

    tallies = jnp.where(number % 4 == 0, named(crowded, number // 4), named(ordinary, number - number // 4 - 1))
    mixed = jax.random.permutation(jax.random.fold_in(own, 3), amount)
    donor, taker = mixed[0:amount // 2 * 2:2], mixed[1:amount // 2 * 2:2]
    slack = jnp.minimum(tallies[donor] - 1, most - tallies[taker]) // 2
    slack = jnp.where((donor == ranking[0]) | (taker == ranking[0]) | (tallies[taker] == 0), 0, jnp.maximum(slack, 0))
    moved = jax.random.randint(jax.random.fold_in(own, 4), (amount // 2,), 0, 1 << 20) % (slack + 1)
    tallies = tallies.at[donor].add(-moved).at[taker].add(moved)
    members = jnp.searchsorted(jnp.cumsum(tallies), jnp.arange(rows * top), side="right").astype(jnp.int32)
    listing = members.reshape(top, rows).T
    listing = listing[jax.random.permutation(jax.random.fold_in(own, 1), rows)]
    turn = jax.random.randint(jax.random.fold_in(own, 2), (rows, 1), 0, top)
    return jnp.take_along_axis(listing, (jnp.arange(top)[None, :] + turn) % top, axis=1)


def load_shares(number_of, total, bound, slope, full):
    loads = [(1 << 20) // math.isqrt(standing ** slope) + 1 for standing in range(1, number_of + 1)]
    largest = bound if full else min(bound, max(-(-total // number_of), total * loads[0] // sum(loads)))
    least = 1 if total - largest >= number_of - 1 else 0
    holding, rest = [largest] + [least] * (number_of - 1), total - largest - least * (number_of - 1)
    while rest > 0:
        free = [i for i in range(1, number_of) if holding[i] < largest] or [i for i in range(1, number_of) if holding[i] < bound]
        pool, left = sum([loads[i] for i in free]), rest
        for i in free:
            extra = min(bound - holding[i], max(1, left * loads[i] // pool), rest)
            holding[i] = holding[i] + extra
            rest = rest - extra
    return np.array(holding)


def centred(stream_key, extent, spread, most, shards=(), held_as=jnp.bfloat16):
    drawn = spread * jax.random.normal(stream_key, extent, jnp.float32)
    if shards:
        drawn = drawn * steps_of(stream_key, extent, shards, -0.22, 0.18)
    return jnp.clip(drawn, -most, most).astype(held_as)


def setup_inputs(seed: int = 0) -> dict:
    seeds = jax.random.split(jax.random.key(seed), 5)
    new_rows = centred(seeds[0], (ROWS, D), 1.0, 6.0, ((0, 16), (1, 8)), jnp.float32)
    old_rows = centred(seeds[1], (ROWS, D), 0.7, 6.0, ((0, 16), (1, 8)), jnp.float32)
    row_ids = touch_ends(jax.random.randint(seeds[2], (ROWS,), 0, TABLE), jax.random.fold_in(seeds[2], 1), 0, TABLE - 1).astype(jnp.int32)
    owner_keys = jax.random.split(jax.random.fold_in(seeds[3], 1), ROWS // BLK)
    owner_turns = jax.random.permutation(jax.random.fold_in(seeds[3], 3), ROWS // BLK)
    owner = jax.vmap(lambda own, number: routed_block(jax.random.fold_in(seeds[3], 2), own, number, BLK, DEVICES, 1, CAP, 2))(owner_keys, owner_turns).reshape((ROWS, 1))
    return dict(new_rows=new_rows, old_rows=old_rows, row_ids=row_ids, owner=owner)


EPSILON = 1e-06

def parity_table(size):
    index_line = lax.iota(jnp.int32, size)
    common_bits = index_line[:, None] & index_line[None, :]
    parity = jnp.zeros_like(common_bits)
    for bit_number in range(max(size.bit_length() - 1, 0)):
        parity = parity ^ common_bits >> bit_number & 1
    return 1 - 2 * parity

def reference(new_rows, old_rows, row_ids, owner):
    devices = N_ROW * N_COL
    block_rows = ROWS_DEV // N_COL
    slice_width = D // N_COL
    capacity = CAP
    inner_table = parity_table(slice_width).astype(jnp.float32)
    outer_table = parity_table(N_COL).astype(jnp.float32)
    scale_factor = 1.0 / math.sqrt(D)
    device_line = lax.iota(jnp.int32, devices)
    owner_flat = owner[:, 0]

    def one_block(block):
        start = (block * block_rows).astype(jnp.int32)
        fresh = lax.dynamic_slice_in_dim(new_rows, start, block_rows, 0)
        stale = lax.dynamic_slice_in_dim(old_rows, start, block_rows, 0)
        delta_low = lax.optimization_barrier((fresh - stale).astype(jnp.bfloat16))
        delta = delta_low.astype(jnp.float32)
        split = delta.reshape(block_rows, N_COL, slice_width)
        inner = jnp.einsum('rab,bc->rac', split, inner_table, precision=lax.Precision.HIGHEST)
        mixed = jnp.einsum('rac,ad->rdc', inner, outer_table, precision=lax.Precision.HIGHEST)
        rotated = mixed.reshape(block_rows, D) * scale_factor
        peak_value = lax.optimization_barrier(jnp.max(jnp.abs(rotated), axis=1))
        codes = (rotated / (peak_value[:, None] + EPSILON)).astype(jnp.bfloat16)
        targets = lax.dynamic_slice_in_dim(owner_flat, start, block_rows, 0)
        marks = (targets[:, None] == device_line[None, :]).astype(jnp.int32)
        slot = lax.optimization_barrier(jnp.sum(marks * jnp.cumsum(marks, axis=0), axis=1)) - 1
        place = targets * (devices * capacity) + block * capacity + slot
        return (codes, peak_value.astype(jnp.bfloat16), place.astype(jnp.int32))
    codes, scales, places = lax.map(one_block, jnp.arange(devices, dtype=jnp.int32))
    total = devices * devices * capacity
    flat_places = places.reshape(-1)
    published = jnp.zeros((total, D), jnp.bfloat16).at[flat_places].set(codes.reshape(-1, D))
    row_scale = jnp.zeros((total,), jnp.bfloat16).at[flat_places].set(scales.reshape(-1))
    published_ids = jnp.full((total,), -1, jnp.int32).at[flat_places].set(row_ids)
    return (published, row_scale, published_ids)
```

```python
import functools
import math

import jax
import jax.numpy as jnp
from jax import lax
from jax.experimental import pallas as pl
from jax.experimental.pallas import tpu as pltpu
from jax.sharding import PartitionSpec as P

EPSILON = 1e-06
MESH = pl.DeviceIdType.MESH
BF16, F32, I32 = jnp.bfloat16, jnp.float32, jnp.int32

N_ROW, N_COL = 16, 8
DEVICES = N_ROW * N_COL
CAP = 4
BLK = 256
SLICE = 256
D = SLICE * N_COL
ROWS_HERE = BLK * N_COL
CHUNK = CAP * N_COL
SLOTS = CHUNK * N_ROW
PAIRS = N_COL // 2
BATCH = 4


def parity_signs(size):
    common = lax.broadcasted_iota(I32, (size, size), 0) & lax.broadcasted_iota(I32, (size, size), 1)
    for shift in (4, 2, 1):
        common = common ^ (common >> shift)
    return (1 - 2 * (common & 1)).astype(F32).astype(BF16)


def kernel(
    new_ref, old_ref, owner_ref, ids_ref,
    out_ref, scale_ref, oid_ref,
    fresh, stale, delta, send, recv, codes, peaks, table, ids_send, ids_recv,
    load_sem, send_sem, recv_sem, self_sem, ids_send_sem, ids_recv_sem, ids_self_sem, out_sem,
):
    row = lax.axis_index("row")
    col = lax.axis_index("col")
    y, x = row // 4, row % 4
    z, core = col // 2, col % 2

    def ahead(step):
        return ((y + step // 4) % 4) * 4 + (x + step % 4) % 4

    def behind(step):
        return ((y + 4 - step // 4) % 4) * 4 + (x + 4 - step % 4) % 4

    def column(step):
        return ((z + step // 2) % 4) * 2 + (core + step) % 2

    def loads(pair):
        part = pl.ds(pair * 2 * BLK, 2 * BLK)
        return (
            pltpu.make_async_copy(new_ref.at[part], fresh.at[part], load_sem.at[pair]),
            pltpu.make_async_copy(old_ref.at[part], stale.at[part], load_sem.at[pair + PAIRS]),
        )

    for pair in range(PAIRS):
        for copy in loads(pair):
            copy.start()

    barrier = pltpu.get_barrier_semaphore()

    def greet(number, _):
        pl.semaphore_signal(
            barrier, inc=1, device_id=(ahead(number // N_COL), column(number % N_COL)), device_id_type=MESH
        )
        return 0

    lax.fori_loop(1, DEVICES, greet, 0)

    owner_lines = []
    marks = []
    for block in range(N_COL):
        line = jnp.concatenate([owner_ref[2 * block:2 * block + 1, :], owner_ref[2 * block + 1:2 * block + 2, :]], axis=1)
        owner_lines.append(line)
        marks.append(jnp.where(lax.broadcasted_iota(I32, (DEVICES, BLK), 0) == line, 1.0, 0.0))
    earlier = jnp.where(
        lax.broadcasted_iota(I32, (BLK, BLK), 0) < lax.broadcasted_iota(I32, (BLK, BLK), 1), 1.0, 0.0
    ).astype(BF16)
    slots = []
    for block in range(N_COL):
        counts = jnp.dot(marks[block].astype(BF16), earlier, preferred_element_type=F32)
        slots.append(jnp.sum(marks[block] * counts, axis=0, keepdims=True).astype(I32))
    keys = []
    for pair in range(PAIRS):
        first, second = 2 * pair, 2 * pair + 1
        keys.append(jnp.concatenate(
            [owner_lines[first] * (2 * CAP) + slots[first], owner_lines[second] * (2 * CAP) + CAP + slots[second]], axis=1
        ))

    for pair in range(PAIRS):
        for copy in loads(pair):
            copy.wait()
        part = pl.ds(pair * 2 * BLK, 2 * BLK)
        delta[part, :] = (fresh[part, :] - stale[part, :]).astype(BF16)

    pl.semaphore_wait(barrier, DEVICES - 1)

    def chunk_copy(step, other):
        return pltpu.make_async_remote_copy(
            src_ref=send.at[step * N_COL + other],
            dst_ref=recv.at[col, pl.ds(row * CHUNK, CHUNK)],
            send_sem=send_sem,
            recv_sem=recv_sem.at[step],
            device_id=(ahead(step), column(other)),
            device_id_type=MESH,
        )

    self_copy = pltpu.make_async_copy(send.at[0], recv.at[col, pl.ds(row * CHUNK, CHUNK)], self_sem)
    span = N_COL * 2 * CAP
    for batch in range(N_ROW // BATCH):
        packed = []
        for pair in range(PAIRS):
            picks = []
            for inner in range(BATCH):
                base = ahead(batch * BATCH + inner) * span
                line = lax.broadcasted_iota(I32, (span, 2 * BLK), 0)
                step = line // (2 * CAP)
                there = ((z + step // 2) % 4) * 2 + (core + step) % 2
                target = base + there * (2 * CAP) + line % (2 * CAP)
                picks.append(jnp.where(target == keys[pair], 1.0, 0.0).astype(BF16))
            rows = jnp.dot(
                jnp.concatenate(picks, axis=0), delta[pair * 2 * BLK:(pair + 1) * 2 * BLK, :], preferred_element_type=F32
            )
            packed.append(rows.reshape(BATCH * N_COL, 2 * CAP, SLICE))
        for half in range(PAIRS // 2):
            send[batch * BATCH * N_COL:(batch + 1) * BATCH * N_COL, half * 16:(half + 1) * 16, :] = jnp.concatenate(
                [packed[2 * half], packed[2 * half + 1]], axis=1
            ).astype(BF16)

        def start(number, _):
            chunk_copy(number // N_COL, number % N_COL).start()
            return 0

        if batch == 0:
            self_copy.start()
            lax.fori_loop(1, BATCH * N_COL, start, 0)
        else:
            lax.fori_loop(batch * BATCH * N_COL, (batch + 1) * BATCH * N_COL, start, 0)

    all_owners = jnp.concatenate(owner_lines, axis=1)
    all_slots = jnp.concatenate(slots, axis=1)
    lane = lax.broadcasted_iota(I32, (1, ROWS_HERE), 1)
    place = (row % 4) * CHUNK + (lane // BLK) * CAP + all_slots
    at_place = jnp.where(lax.broadcasted_iota(I32, (128, ROWS_HERE), 0) == place, 1.0, 0.0).astype(BF16)
    values = jnp.concatenate([ids_ref[i:i + 1, :] for i in range(ROWS_HERE // 128)], axis=1) + 1
    group = lax.broadcasted_iota(I32, (N_ROW, ROWS_HERE), 0)
    there = ((y + group // 4) % 4) * 4 + (x + group % 4) % 4
    mine = all_owners == there * N_COL + col
    pieces = [jnp.where(mine, part.astype(F32), 0.0).astype(BF16) for part in (values >> 16, (values >> 8) & 255, values & 255)]
    sums = lax.dot_general(
        jnp.concatenate(pieces, axis=0), at_place, (((1,), (1,)), ((), ())), preferred_element_type=F32
    )
    found = (sums[:N_ROW] * 65536.0 + sums[N_ROW:2 * N_ROW] * 256.0 + sums[2 * N_ROW:]).astype(I32)
    for step in range(N_ROW):
        ids_send[step] = found[step:step + 1, :]

    def ids_copy(step):
        return pltpu.make_async_remote_copy(
            src_ref=ids_send.at[step],
            dst_ref=ids_recv.at[row],
            send_sem=ids_send_sem,
            recv_sem=ids_recv_sem,
            device_id=(ahead(step), col),
            device_id_type=MESH,
        )

    ids_self = pltpu.make_async_copy(ids_send.at[0], ids_recv.at[row], ids_self_sem)
    ids_self.start()

    def start_ids(step, _):
        ids_copy(step).start()
        return 0

    lax.fori_loop(1, N_ROW, start_ids, 0)

    table[...] = parity_signs(SLICE)

    def out_copy(source):
        part = pl.ds(source * CHUNK, CHUNK)
        return pltpu.make_async_copy(codes.at[part], out_ref.at[part], out_sem)

    def rotate(step):
        source = behind(step)
        part = pl.ds(pl.multiple_of(source * CHUNK, CHUNK), CHUNK)
        got = recv[:, part, :].reshape(N_COL * CHUNK, SLICE)
        inner = jnp.dot(got, table[...], preferred_element_type=F32)
        lines = [inner[c * CHUNK:(c + 1) * CHUNK] for c in range(N_COL)]
        for gap in (1, 2, 4):
            lines = [
                lines[c] + lines[c + gap] if not c & gap else lines[c - gap] - lines[c] for c in range(N_COL)
            ]
        top = functools.reduce(jnp.maximum, [jnp.abs(line) for line in lines])
        peak = jnp.max(top, axis=1, keepdims=True) * (1.0 / math.sqrt(D))
        peaks[part, :] = jnp.broadcast_to(peak, (CHUNK, 128))
        factor = (1.0 / math.sqrt(D)) / (peak + EPSILON)
        for c in range(N_COL):
            codes[part, c * SLICE:(c + 1) * SLICE] = (lines[c] * factor).astype(BF16)
        out_copy(source).start()

    pltpu.make_async_copy(send.at[pl.ds(0, N_COL - 1)], send.at[pl.ds(0, N_COL - 1)], recv_sem.at[0]).wait()
    self_copy.wait()
    rotate(0)

    def turn(step, _):
        part = pl.ds(0, N_COL)
        pltpu.make_async_copy(send.at[part], send.at[part], recv_sem.at[step]).wait()
        rotate(step)
        return 0

    lax.fori_loop(1, N_ROW, turn, 0)

    diagonal = lax.broadcasted_iota(I32, (128, 128), 0) == lax.broadcasted_iota(I32, (128, 128), 1)
    for q in range(SLOTS // 128):
        scale_ref[q:q + 1, :] = jnp.sum(jnp.where(diagonal, peaks[q * 128:(q + 1) * 128, :], 0.0), axis=0, keepdims=True)

    ids_self.wait()
    others = pl.ds(0, N_ROW - 1)
    pltpu.make_async_copy(ids_send.at[others], ids_send.at[others], ids_recv_sem).wait()
    for q in range(SLOTS // 128):
        oid_ref[q:q + 1, :] = ids_recv[4 * q] + ids_recv[4 * q + 1] + ids_recv[4 * q + 2] + ids_recv[4 * q + 3] - 1

    pltpu.make_async_copy(codes, out_ref, out_sem).wait()
    everyone = pl.ds(0, DEVICES - 1)
    pltpu.make_async_copy(send.at[everyone], send.at[everyone], send_sem).wait()
    pltpu.make_async_copy(ids_send.at[others], ids_send.at[others], ids_send_sem).wait()


def shards(new_rows, old_rows, row_ids, owner):
    vmem = pl.BlockSpec(memory_space=pltpu.VMEM)
    anywhere = pl.BlockSpec(memory_space=pl.ANY)
    published, scale, ids = pl.pallas_call(
        kernel,
        out_shape=(
            jax.ShapeDtypeStruct((SLOTS, D), BF16),
            jax.ShapeDtypeStruct((SLOTS // 128, 128), F32),
            jax.ShapeDtypeStruct((SLOTS // 128, 128), I32),
        ),
        in_specs=[anywhere, anywhere, vmem, vmem],
        out_specs=(anywhere, vmem, vmem),
        scratch_shapes=[
            pltpu.VMEM((ROWS_HERE, SLICE), F32),
            pltpu.VMEM((ROWS_HERE, SLICE), F32),
            pltpu.VMEM((ROWS_HERE, SLICE), BF16),
            pltpu.VMEM((DEVICES, CHUNK, SLICE), BF16),
            pltpu.VMEM((N_COL, SLOTS, SLICE), BF16),
            pltpu.VMEM((SLOTS, D), BF16),
            pltpu.VMEM((SLOTS, 128), F32),
            pltpu.VMEM((SLICE, SLICE), BF16),
            pltpu.VMEM((N_ROW, 1, 128), I32),
            pltpu.VMEM((N_ROW, 1, 128), I32),
            pltpu.SemaphoreType.DMA((2 * PAIRS,)),
            pltpu.SemaphoreType.DMA,
            pltpu.SemaphoreType.DMA((N_ROW,)),
            pltpu.SemaphoreType.DMA,
            pltpu.SemaphoreType.DMA,
            pltpu.SemaphoreType.DMA,
            pltpu.SemaphoreType.DMA,
            pltpu.SemaphoreType.DMA,
        ],
        compiler_params=pltpu.CompilerParams(
            collective_id=0, has_side_effects=True, vmem_limit_bytes=40 * 1024 * 1024
        ),
    )(new_rows, old_rows, owner.reshape(ROWS_HERE // 128, 128), row_ids.reshape(ROWS_HERE // 128, 128))
    return published, scale.reshape(SLOTS).astype(BF16), ids.reshape(SLOTS)


def solution(mesh):
    return jax.shard_map(
        shards,
        mesh=mesh,
        in_specs=(P("row", "col"), P("row", "col"), P("row"), P("row", None)),
        out_specs=(P(("row", "col"), None), P(("row", "col")), P(("row", "col"))),
        check_vma=False,
    )
```

```python
import functools
import math

import jax
import jax.numpy as jnp
from jax import lax
from jax.experimental import pallas as pl
from jax.experimental.pallas import tpu as pltpu
from jax.sharding import PartitionSpec as P

EPSILON = 1e-06
MESH = pl.DeviceIdType.MESH
BF16, F32, I32 = jnp.bfloat16, jnp.float32, jnp.int32

N_ROW, N_COL = 16, 8
DEVICES = N_ROW * N_COL
CAP = 4
BLK = 256
SLICE = 256
D = SLICE * N_COL
ROWS_HERE = BLK * N_COL
CHUNK = CAP * N_COL
SLOTS = CHUNK * N_ROW
PAIRS = N_COL // 2


def parity_signs(size):
    common = lax.broadcasted_iota(I32, (size, size), 0) & lax.broadcasted_iota(I32, (size, size), 1)
    for shift in (4, 2, 1):
        common = common ^ (common >> shift)
    return (1 - 2 * (common & 1)).astype(F32).astype(BF16)


UNITS = (
    ((1, 1), (3, 3)),
    ((1, 3), (3, 1)),
    ((1, 2), (3, 2), (1, 0), (3, 0)),
    ((2, 1), (2, 3), (0, 1), (0, 3)),
    ((0, 2), (2, 0)),
    ((2, 2), (0, 0)),
)
SPAN = N_COL * 2 * CAP


def kernel(
    new_ref, old_ref, owner_hbm, ids_hbm,
    out_ref, scale_ref, oid_ref,
    fresh, stale, owner_ref, ids_ref, delta, send, recv, codes, peaks, table, ids_send, ids_recv,
    load_sem, small_sem, plane_sem, cube_sem,
    send_sem, recv_sem, self_sem, ids_send_sem, ids_recv_sem, ids_self_sem, out_sem,
):
    row = lax.axis_index("row")
    col = lax.axis_index("col")
    y, x = row // 4, row % 4
    z, core = col // 2, col % 2

    def ahead(group):
        return ((y + group[0]) % 4) * 4 + (x + group[1]) % 4

    def behind(group):
        return ((y + 4 - group[0]) % 4) * 4 + (x + 4 - group[1]) % 4

    def column(step):
        return ((z + step // 2) % 4) * 2 + (core + step) % 2

    def loads(pair):
        part = pl.ds(pair * 2 * BLK, 2 * BLK)
        return (
            pltpu.make_async_copy(new_ref.at[part], fresh.at[part], load_sem.at[pair]),
            pltpu.make_async_copy(old_ref.at[part], stale.at[part], load_sem.at[pair + PAIRS]),
        )

    owner_load = pltpu.make_async_copy(owner_hbm, owner_ref, small_sem.at[0])
    ids_load = pltpu.make_async_copy(ids_hbm, ids_ref, small_sem.at[1])
    owner_load.start()
    for pair in range(PAIRS):
        for copy in loads(pair):
            copy.start()
    ids_load.start()

    barrier = pltpu.get_barrier_semaphore()
    along_x = [(ahead((0, step)), col) for step in (1, 2, 3)]
    along_y = [(ahead((step, 0)), col) for step in (1, 2, 3)]
    along_col = [(row, column(step)) for step in range(1, N_COL)]
    for device in along_col + along_x + along_y:
        pl.semaphore_signal(barrier, inc=1, device_id=device, device_id_type=MESH)

    owner_load.wait()
    owner_lines = []
    marks = []
    for block in range(N_COL):
        line = jnp.concatenate([owner_ref[2 * block:2 * block + 1, :], owner_ref[2 * block + 1:2 * block + 2, :]], axis=1)
        owner_lines.append(line)
        marks.append(jnp.where(lax.broadcasted_iota(I32, (DEVICES, BLK), 0) == line, 1.0, 0.0))
    earlier = jnp.where(
        lax.broadcasted_iota(I32, (BLK, BLK), 0) < lax.broadcasted_iota(I32, (BLK, BLK), 1), 1.0, 0.0
    ).astype(BF16)
    slots = []
    for block in range(N_COL):
        counts = jnp.dot(marks[block].astype(BF16), earlier, preferred_element_type=F32)
        slots.append(jnp.sum(marks[block] * counts, axis=0, keepdims=True).astype(I32))
    keys = []
    for pair in range(PAIRS):
        halves = []
        for half in range(2):
            line = owner_lines[2 * pair + half]
            group_step = ((line // 32 + 4 - y) % 4) * 4 + (line // N_COL + 4 - x) % 4
            col_step = ((line // 2 + 4 - z) % 4) * 2 + (line + core) % 2
            halves.append((group_step * N_COL + col_step) * (2 * CAP) + half * CAP + slots[2 * pair + half])
        keys.append(jnp.concatenate(halves, axis=1))

    pl.semaphore_wait(barrier, len(along_col + along_x + along_y))
    for device in along_x:
        pl.semaphore_signal(plane_sem, inc=1, device_id=device, device_id_type=MESH)

    for pair in range(PAIRS):
        for copy in loads(pair):
            copy.wait()
        part = pl.ds(pair * 2 * BLK, 2 * BLK)
        delta[part, :] = (fresh[part, :] - stale[part, :]).astype(BF16)

    pl.semaphore_wait(plane_sem, len(along_x))
    for device in along_y:
        pl.semaphore_signal(cube_sem, inc=1, device_id=device, device_id_type=MESH)

    def chunk_copy(group, index, step):
        return pltpu.make_async_remote_copy(
            src_ref=send.at[index * N_COL + step],
            dst_ref=recv.at[col, pl.ds(row * CHUNK, CHUNK)],
            send_sem=send_sem,
            recv_sem=recv_sem.at[index],
            device_id=(ahead(group), column(step)),
            device_id_type=MESH,
        )

    order = [group for unit in UNITS for group in unit]
    own = order.index((0, 0))
    self_copy = pltpu.make_async_copy(send.at[own * N_COL], recv.at[col, pl.ds(row * CHUNK, CHUNK)], self_sem)
    lines = lax.broadcasted_iota(I32, (SPAN, 2 * BLK), 0)
    index = 0
    for unit in UNITS:
        packed = []
        for pair in range(PAIRS):
            picks = [
                jnp.where(lines == keys[pair] - (group[0] * 4 + group[1]) * SPAN, 1.0, 0.0).astype(BF16) for group in unit
            ]
            rows = jnp.dot(
                jnp.concatenate(picks, axis=0), delta[pair * 2 * BLK:(pair + 1) * 2 * BLK, :], preferred_element_type=F32
            )
            packed.append(rows.reshape(len(unit) * N_COL, 2 * CAP, SLICE))
        for half in range(PAIRS // 2):
            send[index * N_COL:(index + len(unit)) * N_COL, half * 16:(half + 1) * 16, :] = jnp.concatenate(
                [packed[2 * half], packed[2 * half + 1]], axis=1
            ).astype(BF16)

        if index == 0:
            pl.semaphore_wait(cube_sem, len(along_y))

        def start(number, _, unit=unit, index=index):
            for place, group in enumerate(unit):
                step = (3 * number + 2 * place + 2) % N_COL
                if group == (0, 0):
                    @pl.when(step != 0)
                    def _():
                        chunk_copy(group, index + place, step).start()
                else:
                    chunk_copy(group, index + place, step).start()
            return 0

        lax.fori_loop(0, N_COL, start, 0)
        if (0, 0) in unit:
            self_copy.start()
        index += len(unit)

    ids_load.wait()
    all_owners = jnp.concatenate(owner_lines, axis=1)
    all_slots = jnp.concatenate(slots, axis=1)
    lane = lax.broadcasted_iota(I32, (1, ROWS_HERE), 1)
    place = (row % 4) * CHUNK + (lane // BLK) * CAP + all_slots
    at_place = jnp.where(lax.broadcasted_iota(I32, (128, ROWS_HERE), 0) == place, 1.0, 0.0).astype(BF16)
    values = jnp.concatenate([ids_ref[i:i + 1, :] for i in range(ROWS_HERE // 128)], axis=1) + 1
    number = lax.broadcasted_iota(I32, (N_ROW, ROWS_HERE), 0)
    there = ((y + number // 4) % 4) * 4 + (x + number % 4) % 4
    mine = all_owners == there * N_COL + col
    pieces = [jnp.where(mine, part.astype(F32), 0.0).astype(BF16) for part in (values >> 16, (values >> 8) & 255, values & 255)]
    sums = lax.dot_general(
        jnp.concatenate(pieces, axis=0), at_place, (((1,), (1,)), ((), ())), preferred_element_type=F32
    )
    found = (sums[:N_ROW] * 65536.0 + sums[N_ROW:2 * N_ROW] * 256.0 + sums[2 * N_ROW:]).astype(I32)
    for step in range(N_ROW):
        ids_send[step] = found[step:step + 1, :]

    ids_self = pltpu.make_async_copy(ids_send.at[0], ids_recv.at[row], ids_self_sem)
    ids_self.start()

    def start_ids(step, _):
        pltpu.make_async_remote_copy(
            src_ref=ids_send.at[step],
            dst_ref=ids_recv.at[row],
            send_sem=ids_send_sem,
            recv_sem=ids_recv_sem,
            device_id=(ahead((step // 4, step % 4)), col),
            device_id_type=MESH,
        ).start()
        return 0

    lax.fori_loop(1, N_ROW, start_ids, 0)

    table[...] = parity_signs(SLICE)

    def rotate(source):
        part = pl.ds(pl.multiple_of(source * CHUNK, CHUNK), CHUNK)
        got = recv[:, part, :].reshape(N_COL * CHUNK, SLICE)
        inner = jnp.dot(got, table[...], preferred_element_type=F32)
        lines = [inner[c * CHUNK:(c + 1) * CHUNK] for c in range(N_COL)]
        for gap in (1, 2, 4):
            lines = [
                lines[c] + lines[c + gap] if not c & gap else lines[c - gap] - lines[c] for c in range(N_COL)
            ]
        top = functools.reduce(jnp.maximum, [jnp.abs(line) for line in lines])
        peak = jnp.max(top, axis=1, keepdims=True) * (1.0 / math.sqrt(D))
        peaks[part, :] = jnp.broadcast_to(peak, (CHUNK, 128))
        factor = (1.0 / math.sqrt(D)) / (peak + EPSILON)
        for c in range(N_COL):
            codes[part, c * SLICE:(c + 1) * SLICE] = (lines[c] * factor).astype(BF16)
        pltpu.make_async_copy(codes.at[part], out_ref.at[part], out_sem).start()

    for index, group in enumerate(order):
        chunks = pl.ds(0, N_COL - 1 if index == own else N_COL)
        pltpu.make_async_copy(send.at[chunks], send.at[chunks], recv_sem.at[index]).wait()
        if index == own:
            self_copy.wait()
        rotate(behind(group))

    diagonal = lax.broadcasted_iota(I32, (128, 128), 0) == lax.broadcasted_iota(I32, (128, 128), 1)
    for q in range(SLOTS // 128):
        scale_ref[q:q + 1, :] = jnp.sum(jnp.where(diagonal, peaks[q * 128:(q + 1) * 128, :], 0.0), axis=0, keepdims=True)

    ids_self.wait()
    others = pl.ds(0, N_ROW - 1)
    pltpu.make_async_copy(ids_send.at[others], ids_send.at[others], ids_recv_sem).wait()
    for q in range(SLOTS // 128):
        oid_ref[q:q + 1, :] = ids_recv[4 * q] + ids_recv[4 * q + 1] + ids_recv[4 * q + 2] + ids_recv[4 * q + 3] - 1

    pltpu.make_async_copy(codes, out_ref, out_sem).wait()
    everyone = pl.ds(0, DEVICES - 1)
    pltpu.make_async_copy(send.at[everyone], send.at[everyone], send_sem).wait()
    pltpu.make_async_copy(ids_send.at[others], ids_send.at[others], ids_send_sem).wait()


def shards(new_rows, old_rows, row_ids, owner):
    vmem = pl.BlockSpec(memory_space=pltpu.VMEM)
    anywhere = pl.BlockSpec(memory_space=pl.ANY)
    published, scale, ids = pl.pallas_call(
        kernel,
        out_shape=(
            jax.ShapeDtypeStruct((SLOTS, D), BF16),
            jax.ShapeDtypeStruct((SLOTS // 128, 128), F32),
            jax.ShapeDtypeStruct((SLOTS // 128, 128), I32),
        ),
        in_specs=[anywhere] * 4,
        out_specs=(anywhere, vmem, vmem),
        scratch_shapes=[
            pltpu.VMEM((ROWS_HERE, SLICE), F32),
            pltpu.VMEM((ROWS_HERE, SLICE), F32),
            pltpu.VMEM((ROWS_HERE // 128, 128), I32),
            pltpu.VMEM((ROWS_HERE // 128, 128), I32),
            pltpu.VMEM((ROWS_HERE, SLICE), BF16),
            pltpu.VMEM((DEVICES, CHUNK, SLICE), BF16),
            pltpu.VMEM((N_COL, SLOTS, SLICE), BF16),
            pltpu.VMEM((SLOTS, D), BF16),
            pltpu.VMEM((SLOTS, 128), F32),
            pltpu.VMEM((SLICE, SLICE), BF16),
            pltpu.VMEM((N_ROW, 1, 128), I32),
            pltpu.VMEM((N_ROW, 1, 128), I32),
            pltpu.SemaphoreType.DMA((2 * PAIRS,)),
            pltpu.SemaphoreType.DMA((2,)),
            pltpu.SemaphoreType.REGULAR,
            pltpu.SemaphoreType.REGULAR,
            pltpu.SemaphoreType.DMA,
            pltpu.SemaphoreType.DMA((N_ROW,)),
            pltpu.SemaphoreType.DMA,
            pltpu.SemaphoreType.DMA,
            pltpu.SemaphoreType.DMA,
            pltpu.SemaphoreType.DMA,
            pltpu.SemaphoreType.DMA,
        ],
        compiler_params=pltpu.CompilerParams(
            collective_id=0, has_side_effects=True, vmem_limit_bytes=40 * 1024 * 1024
        ),
    )(*(
        pltpu.with_memory_space_constraint(array, pltpu.HBM)
        for array in (new_rows, old_rows, owner.reshape(ROWS_HERE // 128, 128), row_ids.reshape(ROWS_HERE // 128, 128))
    ))
    return published, scale.reshape(SLOTS).astype(BF16), ids.reshape(SLOTS)


def solution(mesh):
    return jax.shard_map(
        shards,
        mesh=mesh,
        in_specs=(P("row", "col"), P("row", "col"), P("row"), P("row", None)),
        out_specs=(P(("row", "col"), None), P(("row", "col")), P(("row", "col"))),
        check_vma=False,
    )
```

```python
import functools
import math
import random

import jax
import jax.numpy as jnp
from jax import lax
from jax.experimental import pallas as pl
from jax.experimental.pallas import tpu as pltpu
from jax.sharding import PartitionSpec as P

EPSILON = 1e-06
MESH = pl.DeviceIdType.MESH
BF16, F32, I32 = jnp.bfloat16, jnp.float32, jnp.int32

N_ROW, N_COL = 16, 8
DEVICES = N_ROW * N_COL
CAP = 4
BLK = 256
SLICE = 256
D = SLICE * N_COL
ROWS_HERE = BLK * N_COL
CHUNK = CAP * N_COL
SLOTS = CHUNK * N_ROW
PAIRS = N_COL // 2


def parity_signs(size):
    common = lax.broadcasted_iota(I32, (size, size), 0) & lax.broadcasted_iota(I32, (size, size), 1)
    for shift in (4, 2, 1):
        common = common ^ (common >> shift)
    return (1 - 2 * (common & 1)).astype(F32).astype(BF16)


def hops(chunk):
    used = []
    for step in (chunk[0] % 4, chunk[0] // 4, chunk[1] // 2):
        used += [(0, 0), (1, 0), (1, 1), (0, 1)][step]
    return used


def balanced(chunks, seed):
    rest, done, order = list(chunks), [0] * 6, []
    random.Random(seed).shuffle(rest)
    total = [max(1, sum(hops(chunk)[link] for chunk in chunks)) for link in range(6)]
    while rest:
        part = (len(order) + 1) / len(chunks)
        best = min(rest, key=lambda chunk: sum(((d + h) / t - part) ** 2 for d, h, t in zip(done, hops(chunk), total)))
        rest.remove(best)
        order.append(best)
        done = [d + h for d, h in zip(done, hops(best))]
    return order


WINDOWS = ((1, 4, 11, 14), (2, 7, 8, 13), (3, 6, 9, 12), (5, 15, 0, 10))
ARRIVAL = [group for window in WINDOWS for group in window]
BATCH = 4
SPAN = N_COL * 2 * CAP


def kernel(
    new_ref, old_ref, owner_hbm, ids_hbm,
    codes, scale_ref, oid_ref,
    fresh, stale, owner_ref, ids_ref, delta, send, recv, peaks, table, ids_send, ids_recv,
    load_sem, small_sem, x_sem, y_sem,
    send_sem, recv_sem, self_sem, ids_send_sem, ids_recv_sem, ids_self_sem,
):
    row = lax.axis_index("row")
    col = lax.axis_index("col")
    y, x = row // 4, row % 4
    z, core = col // 2, col % 2

    def flip(place, step):
        return (place, place + 1 - 2 * (place % 2), (place + 2) % 4, 3 - place)[step]

    def partner(group, step):
        return (flip(y, group // 4) * 4 + flip(x, group % 4), flip(z, step // 2) * 2 + (core + step) % 2)

    def loads(pair):
        part = pl.ds(pair * 2 * BLK, 2 * BLK)
        return (
            pltpu.make_async_copy(new_ref.at[part], fresh.at[part], load_sem.at[pair]),
            pltpu.make_async_copy(old_ref.at[part], stale.at[part], load_sem.at[pair + PAIRS]),
        )

    owner_load = pltpu.make_async_copy(owner_hbm, owner_ref, small_sem.at[0])
    ids_load = pltpu.make_async_copy(ids_hbm, ids_ref, small_sem.at[1])
    owner_load.start()
    for pair in range(PAIRS):
        for copy in loads(pair):
            copy.start()
    ids_load.start()

    barrier = pltpu.get_barrier_semaphore()
    along_x, along_y = (1, 2, 3), (4, 8, 12)

    def tell(sem, groups):
        for group in groups:
            pl.semaphore_signal(sem, inc=1, device_id=partner(group, 0), device_id_type=MESH)

    tell(barrier, along_x + along_y)
    for step in range(1, N_COL):
        pl.semaphore_signal(barrier, inc=1, device_id=partner(0, step), device_id_type=MESH)

    pl.semaphore_wait(barrier, len(along_x + along_y) + N_COL - 1)
    tell(x_sem, along_x)

    owner_load.wait()
    owner_lines = []
    marks = []
    for block in range(N_COL):
        line = jnp.concatenate([owner_ref[2 * block:2 * block + 1, :], owner_ref[2 * block + 1:2 * block + 2, :]], axis=1)
        owner_lines.append(line)
        marks.append(jnp.where(lax.broadcasted_iota(I32, (DEVICES, BLK), 0) == line, 1.0, 0.0))
    earlier = jnp.where(
        lax.broadcasted_iota(I32, (BLK, BLK), 0) < lax.broadcasted_iota(I32, (BLK, BLK), 1), 1.0, 0.0
    ).astype(BF16)
    slots = []
    for block in range(N_COL):
        counts = jnp.dot(marks[block].astype(BF16), earlier, preferred_element_type=F32)
        slots.append(jnp.sum(marks[block] * counts, axis=0, keepdims=True).astype(I32))
    keys = []
    for pair in range(PAIRS):
        halves = []
        for half in range(2):
            line = owner_lines[2 * pair + half]
            group_step = (line // N_COL) ^ row
            col_step = (line % N_COL) ^ col
            position = (((group_step % 4) ^ (group_step // 4)) * 4 + group_step // 4)
            halves.append((position * N_COL + col_step) * (2 * CAP) + half * CAP + slots[2 * pair + half])
        keys.append(jnp.concatenate(halves, axis=1))

    pl.semaphore_wait(x_sem, len(along_x))
    tell(y_sem, along_y)

    for pair in range(PAIRS):
        for copy in loads(pair):
            copy.wait()
        part = pl.ds(pair * 2 * BLK, 2 * BLK)
        delta[part, :] = (fresh[part, :] - stale[part, :]).astype(BF16)

    iota = lax.broadcasted_iota(I32, (BATCH * SPAN, 2 * BLK), 0)

    def pack(window):
        packed = []
        for pair in range(PAIRS):
            picks = jnp.where(iota == keys[pair] - window * BATCH * SPAN, 1.0, 0.0).astype(BF16)
            rows = jnp.dot(picks, delta[pair * 2 * BLK:(pair + 1) * 2 * BLK, :], preferred_element_type=F32)
            packed.append(rows.reshape(BATCH * N_COL, 2 * CAP, SLICE))
        for half in range(PAIRS // 2):
            send[window * BATCH * N_COL:(window + 1) * BATCH * N_COL, half * 16:(half + 1) * 16, :] = jnp.concatenate(
                [packed[2 * half], packed[2 * half + 1]], axis=1
            ).astype(BF16)

    def start(chunks):
        for group, step in chunks:
            position = 4 * ((group % 4) ^ (group // 4)) + group // 4
            pltpu.make_async_remote_copy(
                src_ref=send.at[position * N_COL + step],
                dst_ref=recv.at[col, pl.ds(row * CHUNK, CHUNK)],
                send_sem=send_sem,
                recv_sem=recv_sem.at[group],
                device_id=partner(group, step),
                device_id_type=MESH,
            ).start()

    pack(1)
    pack(2)
    pl.semaphore_wait(y_sem, len(along_y))
    for number, window in enumerate(WINDOWS):
        if number > 1:
            pack((number + 1) % 4)
        start(balanced([(group, step) for group in window for step in range(N_COL) if group or step], 11 + number))
    self_copy = pltpu.make_async_copy(send.at[0], recv.at[col, pl.ds(row * CHUNK, CHUNK)], self_sem)
    self_copy.start()

    ids_load.wait()
    all_owners = jnp.concatenate(owner_lines, axis=1)
    all_slots = jnp.concatenate(slots, axis=1)
    lane = lax.broadcasted_iota(I32, (1, ROWS_HERE), 1)
    place = (row % 4) * CHUNK + (lane // BLK) * CAP + all_slots
    at_place = jnp.where(lax.broadcasted_iota(I32, (128, ROWS_HERE), 0) == place, 1.0, 0.0).astype(BF16)
    values = jnp.concatenate([ids_ref[i:i + 1, :] for i in range(ROWS_HERE // 128)], axis=1) + 1
    number = lax.broadcasted_iota(I32, (N_ROW, ROWS_HERE), 0)
    there = number ^ row
    mine = all_owners == there * N_COL + col
    pieces = [jnp.where(mine, part.astype(F32), 0.0).astype(BF16) for part in (values >> 16, (values >> 8) & 255, values & 255)]
    sums = lax.dot_general(
        jnp.concatenate(pieces, axis=0), at_place, (((1,), (1,)), ((), ())), preferred_element_type=F32
    )
    found = (sums[:N_ROW] * 65536.0 + sums[N_ROW:2 * N_ROW] * 256.0 + sums[2 * N_ROW:]).astype(I32)
    for step in range(N_ROW):
        ids_send[step] = found[step:step + 1, :]

    ids_self = pltpu.make_async_copy(ids_send.at[0], ids_recv.at[row], ids_self_sem)
    ids_self.start()

    for group in range(1, N_ROW):
        pltpu.make_async_remote_copy(
            src_ref=ids_send.at[group],
            dst_ref=ids_recv.at[row],
            send_sem=ids_send_sem,
            recv_sem=ids_recv_sem,
            device_id=partner(group, 0),
            device_id_type=MESH,
        ).start()

    table[...] = parity_signs(SLICE)

    def rotate(sources):
        parts = [pl.ds(pl.multiple_of(source * CHUNK, CHUNK), CHUNK) for source in sources]
        got = jnp.concatenate([recv[:, part, :] for part in parts], axis=1)
        height = CHUNK * len(sources)
        inner = jnp.dot(got.reshape(N_COL * height, SLICE), table[...], preferred_element_type=F32)
        for place, part in enumerate(parts):
            lines = [inner[c * height + place * CHUNK:c * height + (place + 1) * CHUNK] for c in range(N_COL)]
            for gap in (1, 2, 4):
                lines = [
                    lines[c] + lines[c + gap] if not c & gap else lines[c - gap] - lines[c] for c in range(N_COL)
                ]
            top = functools.reduce(jnp.maximum, [jnp.abs(line) for line in lines])
            peak = jnp.max(top, axis=1, keepdims=True) * (1.0 / math.sqrt(D))
            peaks[part, :] = jnp.broadcast_to(peak, (CHUNK, 128))
            factor = (1.0 / math.sqrt(D)) / (peak + EPSILON)
            for c in range(N_COL):
                codes[part, c * SLICE:(c + 1) * SLICE] = (lines[c] * factor).astype(BF16)

    for first in range(0, N_ROW, 2):
        groups = ARRIVAL[first:first + 2]
        for group in groups:
            chunks = pl.ds(0, N_COL if group else N_COL - 1)
            pltpu.make_async_copy(send.at[chunks], send.at[chunks], recv_sem.at[group]).wait()
            if group == 0:
                self_copy.wait()
        rotate([partner(group, 0)[0] for group in groups])

    diagonal = lax.broadcasted_iota(I32, (128, 128), 0) == lax.broadcasted_iota(I32, (128, 128), 1)
    scale_ref[...] = jnp.concatenate([
        jnp.sum(jnp.where(diagonal, peaks[q * 128:(q + 1) * 128, :], 0.0), axis=0, keepdims=True) for q in range(SLOTS // 128)
    ], axis=0).astype(BF16)

    ids_self.wait()
    others = pl.ds(0, N_ROW - 1)
    pltpu.make_async_copy(ids_send.at[others], ids_send.at[others], ids_recv_sem).wait()
    for q in range(SLOTS // 128):
        oid_ref[q:q + 1, :] = ids_recv[4 * q] + ids_recv[4 * q + 1] + ids_recv[4 * q + 2] + ids_recv[4 * q + 3] - 1

    everyone = pl.ds(0, DEVICES - 1)
    pltpu.make_async_copy(send.at[everyone], send.at[everyone], send_sem).wait()
    pltpu.make_async_copy(ids_send.at[others], ids_send.at[others], ids_send_sem).wait()


def hand_over(codes, scale, ids, published, row_scale, published_ids, sem):
    copies = [
        pltpu.make_async_copy(codes.at[pl.ds(part, SLOTS // 8)], published.at[pl.ds(part, SLOTS // 8)], sem.at[part * 8 // SLOTS])
        for part in range(0, SLOTS, SLOTS // 8)
    ]
    copies += [
        pltpu.make_async_copy(scale, row_scale, sem.at[8]),
        pltpu.make_async_copy(ids, published_ids, sem.at[9]),
    ]
    for copy in copies:
        copy.start()
    for copy in copies:
        copy.wait()


def shards(new_rows, old_rows, row_ids, owner):
    vmem = pl.BlockSpec(memory_space=pltpu.VMEM)
    anywhere = pl.BlockSpec(memory_space=pl.ANY)
    codes, scale, ids = pl.pallas_call(
        kernel,
        out_shape=(
            jax.ShapeDtypeStruct((SLOTS, D), BF16),
            jax.ShapeDtypeStruct((SLOTS // 128, 128), BF16),
            jax.ShapeDtypeStruct((SLOTS // 128, 128), I32),
        ),
        in_specs=[anywhere] * 4,
        out_specs=(vmem, vmem, vmem),
        scratch_shapes=[
            pltpu.VMEM((ROWS_HERE, SLICE), F32),
            pltpu.VMEM((ROWS_HERE, SLICE), F32),
            pltpu.VMEM((ROWS_HERE // 128, 128), I32),
            pltpu.VMEM((ROWS_HERE // 128, 128), I32),
            pltpu.VMEM((ROWS_HERE, SLICE), BF16),
            pltpu.VMEM((DEVICES, CHUNK, SLICE), BF16),
            pltpu.VMEM((N_COL, SLOTS, SLICE), BF16),
            pltpu.VMEM((SLOTS, 128), F32),
            pltpu.VMEM((SLICE, SLICE), BF16),
            pltpu.VMEM((N_ROW, 1, 128), I32),
            pltpu.VMEM((N_ROW, 1, 128), I32),
            pltpu.SemaphoreType.DMA((2 * PAIRS,)),
            pltpu.SemaphoreType.DMA((2,)),
            pltpu.SemaphoreType.REGULAR,
            pltpu.SemaphoreType.REGULAR,
            pltpu.SemaphoreType.DMA,
            pltpu.SemaphoreType.DMA((N_ROW,)),
            pltpu.SemaphoreType.DMA,
            pltpu.SemaphoreType.DMA,
            pltpu.SemaphoreType.DMA,
            pltpu.SemaphoreType.DMA,
        ],
        compiler_params=pltpu.CompilerParams(
            collective_id=0, has_side_effects=True, vmem_limit_bytes=40 * 1024 * 1024
        ),
    )(*(
        pltpu.with_memory_space_constraint(array, pltpu.HBM)
        for array in (new_rows, old_rows, owner.reshape(ROWS_HERE // 128, 128), row_ids.reshape(ROWS_HERE // 128, 128))
    ))
    return pl.pallas_call(
        hand_over,
        out_shape=(
            jax.ShapeDtypeStruct((SLOTS, D), BF16),
            jax.ShapeDtypeStruct((SLOTS,), BF16),
            jax.ShapeDtypeStruct((SLOTS,), I32),
        ),
        in_specs=[anywhere] * 3,
        out_specs=(anywhere,) * 3,
        scratch_shapes=[pltpu.SemaphoreType.DMA((10,))],
        compiler_params=pltpu.CompilerParams(vmem_limit_bytes=1024 * 1024),
    )(*(pltpu.with_memory_space_constraint(array, pltpu.VMEM) for array in (codes, scale.reshape(SLOTS), ids.reshape(SLOTS))))


def solution(mesh):
    return jax.shard_map(
        shards,
        mesh=mesh,
        in_specs=(P("row", "col"), P("row", "col"), P("row"), P("row", None)),
        out_specs=(P(("row", "col"), None), P(("row", "col")), P(("row", "col"))),
        check_vma=False,
    )
```

```python
import functools
import math
import random

import jax
import jax.numpy as jnp
import numpy as np
from jax import lax
from jax.experimental import pallas as pl
from jax.experimental.pallas import tpu as pltpu
from jax.sharding import PartitionSpec as P

EPSILON = 1e-06
MESH = pl.DeviceIdType.MESH
BF16, F32, I32 = jnp.bfloat16, jnp.float32, jnp.int32

N_ROW, N_COL = 16, 8
DEVICES = N_ROW * N_COL
CAP = 4
BLK = 256
SLICE = 256
D = SLICE * N_COL
ROWS_HERE = BLK * N_COL
CHUNK = CAP * N_COL
SLOTS = CHUNK * N_ROW
PAIRS = N_COL // 2


def parity_signs(size):
    common = lax.broadcasted_iota(I32, (size, size), 0) & lax.broadcasted_iota(I32, (size, size), 1)
    for shift in (4, 2, 1):
        common = common ^ (common >> shift)
    return (1 - 2 * (common & 1)).astype(F32).astype(BF16)


def hops(chunk):
    used = []
    for step in (chunk[0] % 4, chunk[0] // 4, chunk[1] // 2):
        used += [(0, 0), (1, 0), (1, 1), (0, 1)][step]
    return used


def balanced(chunks, seed):
    rest, done, order = list(chunks), [0] * 6, []
    random.Random(seed).shuffle(rest)
    total = [max(1, sum(hops(chunk)[link] for chunk in chunks)) for link in range(6)]
    while rest:
        part = (len(order) + 1) / len(chunks)
        best = min(rest, key=lambda chunk: sum(((d + h) / t - part) ** 2 for d, h, t in zip(done, hops(chunk), total)))
        rest.remove(best)
        order.append(best)
        done = [d + h for d, h in zip(done, hops(best))]
    return order


ALL = [(group, step) for group in range(16) for step in range(8) if group or step]
LINES = balanced([(0, step) for step in range(1, 8)] + [(group, 0) for group in (1, 2, 3, 4, 8, 12)], 1)
PLANES = balanced(
    [(group, 0) for group in range(16) if group % 4 and group // 4] + [(group, step) for group in (1, 3, 4, 12) for step in (1, 2, 3, 6, 7)], 2
)
LAST_GROUPS = (5, 15, 7, 13)
LAST = balanced([(group, step) for group in LAST_GROUPS for step in (4, 5, 6, 7)], 3) + balanced(
    [(group, step) for group in LAST_GROUPS for step in (1, 2, 3)], 4
)
FAR = balanced([chunk for chunk in ALL if chunk not in LINES + PLANES + LAST], 5)
ORDER = LINES + PLANES + FAR + LAST
PLACE = {chunk: place for place, chunk in enumerate(ORDER + [(0, 0)])}
ARRIVAL = (0, 1, 3, 4, 12, 2, 8, 6, 9, 10, 11, 14) + LAST_GROUPS
EARLY = 12
BATCH = 32


def flip(place, step):
    return (place, place + 1 - 2 * (place % 2), (place + 2) % 4, 3 - place)[step]


def partner_row(row, group):
    return flip(row // 4, group // 4) * 4 + flip(row % 4, group % 4)


def rotate(recv, table, peaks, codes, sources, targets):
    parts = [pl.ds(pl.multiple_of(source * CHUNK, CHUNK), CHUNK) for source in sources]
    got = jnp.concatenate([recv[:, part, :] for part in parts], axis=1)
    height = CHUNK * len(sources)
    inner = jnp.dot(got.reshape(N_COL * height, SLICE), table[...], preferred_element_type=F32)
    for place, part in enumerate(parts):
        lines = [inner[c * height + place * CHUNK:c * height + (place + 1) * CHUNK] for c in range(N_COL)]
        for gap in (1, 2, 4):
            lines = [lines[c] + lines[c + gap] if not c & gap else lines[c - gap] - lines[c] for c in range(N_COL)]
        top = functools.reduce(jnp.maximum, [jnp.abs(line) for line in lines])
        peak = jnp.max(top, axis=1, keepdims=True) * (1.0 / math.sqrt(D))
        peaks[part, :] = jnp.broadcast_to(peak, (CHUNK, 128))
        factor = (1.0 / math.sqrt(D)) / (peak + EPSILON)
        for c in range(N_COL):
            codes[targets[place], c * SLICE:(c + 1) * SLICE] = (lines[c] * factor).astype(BF16)


def kernel(
    new_ref, old_ref, owner_hbm, ids_hbm, place_hbm,
    codes, recv, peaks, table, ids_recv,
    fresh, stale, owner_ref, ids_ref, place_ref, delta, send, ids_send,
    load_sem, small_sem, x_sem, y_sem, all_sem,
    send_sem, recv_sem, self_sem, ids_send_sem, ids_recv_sem, ids_self_sem,
):
    row = lax.axis_index("row")
    col = lax.axis_index("col")
    y, x = row // 4, row % 4
    z, core = col // 2, col % 2

    def partner(group, step):
        return (partner_row(row, group), flip(z, step // 2) * 2 + (core + step) % 2)

    def loads(pair):
        part = pl.ds(pair * 2 * BLK, 2 * BLK)
        return (
            pltpu.make_async_copy(new_ref.at[part], fresh.at[part], load_sem.at[pair]),
            pltpu.make_async_copy(old_ref.at[part], stale.at[part], load_sem.at[pair + PAIRS]),
        )

    owner_load = pltpu.make_async_copy(owner_hbm, owner_ref, small_sem.at[0])
    ids_load = pltpu.make_async_copy(ids_hbm, ids_ref, small_sem.at[1])
    place_load = pltpu.make_async_copy(place_hbm, place_ref, small_sem.at[2])
    owner_load.start()
    place_load.start()
    for pair in range(PAIRS):
        for copy in loads(pair):
            copy.start()
    ids_load.start()

    barrier = pltpu.get_barrier_semaphore()
    along_x, along_y = (1, 2, 3), (4, 8, 12)

    def tell(sem, groups):
        for group in groups:
            pl.semaphore_signal(sem, inc=1, device_id=partner(group, 0), device_id_type=MESH)

    tell(barrier, along_x + along_y)
    for step in range(1, N_COL):
        pl.semaphore_signal(barrier, inc=1, device_id=partner(0, step), device_id_type=MESH)

    owner_load.wait()
    me = row * N_COL + col
    owner_lines = []
    marks = []
    for block in range(N_COL):
        line = jnp.concatenate([owner_ref[2 * block:2 * block + 1, :], owner_ref[2 * block + 1:2 * block + 2, :]], axis=1) ^ me
        owner_lines.append(line)
        marks.append(jnp.where(lax.broadcasted_iota(I32, (DEVICES, BLK), 0) == line, 1.0, 0.0))
    earlier = jnp.where(
        lax.broadcasted_iota(I32, (BLK, BLK), 0) < lax.broadcasted_iota(I32, (BLK, BLK), 1), 1.0, 0.0
    ).astype(BF16)
    place_load.wait()
    places = jnp.concatenate([place_ref[...]] * (BLK // 128), axis=1)
    slots = []
    keys = []
    for block in range(N_COL):
        counts = jnp.dot(marks[block].astype(BF16), earlier, preferred_element_type=F32)
        slots.append(jnp.sum(marks[block] * counts, axis=0, keepdims=True).astype(I32))
        spot = jnp.sum(marks[block] * (counts + places), axis=0, keepdims=True).astype(I32)
        keys.append(spot + block % 2 * CAP)
    keys = [jnp.concatenate(keys[2 * pair:2 * pair + 2], axis=1) for pair in range(PAIRS)]

    pl.semaphore_wait(barrier, len(LINES))
    tell(x_sem, along_x)
    tell(y_sem, along_y)
    for pair in range(PAIRS):
        for copy in loads(pair):
            copy.wait()
        part = pl.ds(pair * 2 * BLK, 2 * BLK)
        delta[part, :] = (fresh[part, :] - stale[part, :]).astype(BF16)

    iota = lax.broadcasted_iota(I32, (BATCH * 2 * CAP, 2 * BLK), 0)

    def pack(batch):
        packed = []
        for pair in range(PAIRS):
            picks = jnp.where(iota == keys[pair] - batch * BATCH * 2 * CAP, 1.0, 0.0).astype(BF16)
            rows = jnp.dot(picks, delta[pair * 2 * BLK:(pair + 1) * 2 * BLK, :], preferred_element_type=F32)
            packed.append(rows.reshape(BATCH, 2 * CAP, SLICE))
        for half in range(PAIRS // 2):
            send[batch * BATCH:(batch + 1) * BATCH, half * 16:(half + 1) * 16, :] = jnp.concatenate(
                [packed[2 * half], packed[2 * half + 1]], axis=1
            ).astype(BF16)

    def start(first, end):
        for place in range(first, end):
            group, step = ORDER[place]
            pltpu.make_async_remote_copy(
                src_ref=send.at[place],
                dst_ref=recv.at[col, pl.ds(row * CHUNK, CHUNK)],
                send_sem=send_sem,
                recv_sem=recv_sem.at[group],
                device_id=partner(group, step),
                device_id_type=MESH,
            ).start()

    lines, planes = len(LINES), len(LINES + PLANES)
    pack(0)
    start(0, lines)
    pl.semaphore_wait(x_sem, len(along_x))
    tell(all_sem, along_y)
    pack(1)
    pl.semaphore_wait(y_sem, len(along_y))
    start(lines, planes)
    pack(2)
    pl.semaphore_wait(all_sem, len(along_y))
    start(planes, 3 * BATCH)
    pack(3)
    start(3 * BATCH, DEVICES - 1)
    self_copy = pltpu.make_async_copy(send.at[DEVICES - 1], recv.at[col, pl.ds(row * CHUNK, CHUNK)], self_sem)
    self_copy.start()

    ids_load.wait()
    all_owners = jnp.concatenate(owner_lines, axis=1)
    all_slots = jnp.concatenate(slots, axis=1)
    lane = lax.broadcasted_iota(I32, (1, ROWS_HERE), 1)
    place = (row % 4) * CHUNK + (lane // BLK) * CAP + all_slots
    at_place = jnp.where(lax.broadcasted_iota(I32, (128, ROWS_HERE), 0) == place, 1.0, 0.0).astype(BF16)
    values = jnp.concatenate([ids_ref[i:i + 1, :] for i in range(ROWS_HERE // 128)], axis=1) + 1
    number = lax.broadcasted_iota(I32, (N_ROW, ROWS_HERE), 0)
    mine = all_owners == number * N_COL
    pieces = [jnp.where(mine, part.astype(F32), 0.0).astype(BF16) for part in (values >> 16, (values >> 8) & 255, values & 255)]
    sums = lax.dot_general(
        jnp.concatenate(pieces, axis=0), at_place, (((1,), (1,)), ((), ())), preferred_element_type=F32
    )
    found = (sums[:N_ROW] * 65536.0 + sums[N_ROW:2 * N_ROW] * 256.0 + sums[2 * N_ROW:]).astype(I32)
    for step in range(N_ROW):
        ids_send[step] = found[step:step + 1, :]

    ids_self = pltpu.make_async_copy(ids_send.at[0], ids_recv.at[row], ids_self_sem)
    ids_self.start()

    for group in range(1, N_ROW):
        pltpu.make_async_remote_copy(
            src_ref=ids_send.at[group],
            dst_ref=ids_recv.at[row],
            send_sem=ids_send_sem,
            recv_sem=ids_recv_sem,
            device_id=partner(group, 0),
            device_id_type=MESH,
        ).start()

    table[...] = parity_signs(SLICE)

    def arrived(group):
        chunks = pl.ds(0, N_COL if group else N_COL - 1)
        pltpu.make_async_copy(send.at[chunks], send.at[chunks], recv_sem.at[group]).wait()
        if group == 0:
            self_copy.wait()

    for first in range(0, EARLY, 2):
        groups = ARRIVAL[first:first + 2]
        for group in groups:
            arrived(group)
        sources = [partner_row(row, group) for group in groups]
        rotate(recv, table, peaks, codes, sources, [pl.ds(pl.multiple_of(source * CHUNK, CHUNK), CHUNK) for source in sources])
    for group in ARRIVAL[EARLY:]:
        arrived(group)

    ids_self.wait()
    others = pl.ds(0, N_ROW - 1)
    pltpu.make_async_copy(ids_send.at[others], ids_send.at[others], ids_recv_sem).wait()
    everyone = pl.ds(0, DEVICES - 1)
    pltpu.make_async_copy(send.at[everyone], send.at[everyone], send_sem).wait()
    pltpu.make_async_copy(ids_send.at[others], ids_send.at[others], ids_send_sem).wait()


def finish(codes, recv, peaks, table, ids_recv, published, scale_out, ids_out, last_codes, all_peaks, scale_ref, oid_ref, sem):
    row = lax.axis_index("row")

    def slab(source):
        return pl.ds(pl.multiple_of(source * CHUNK, CHUNK), CHUNK)

    copies = []
    for place, group in enumerate(ARRIVAL[:EARLY]):
        part = slab(partner_row(row, group))
        copies.append(pltpu.make_async_copy(codes.at[part], published.at[part], sem.at[place]))
        copies[-1].start()
    for q in range(SLOTS // 128):
        oid_ref[q:q + 1, :] = ids_recv[4 * q] + ids_recv[4 * q + 1] + ids_recv[4 * q + 2] + ids_recv[4 * q + 3] - 1
    copies.append(pltpu.make_async_copy(oid_ref, ids_out, sem.at[N_ROW + 1]))
    copies[-1].start()
    all_peaks[...] = peaks[...]
    for first in range(EARLY, N_ROW, 2):
        sources = [partner_row(row, group) for group in ARRIVAL[first:first + 2]]
        targets = [pl.ds((first - EARLY + place) * CHUNK, CHUNK) for place in range(2)]
        rotate(recv, table, all_peaks, last_codes, sources, targets)
        for place in range(2):
            copies.append(
                pltpu.make_async_copy(last_codes.at[targets[place]], published.at[slab(sources[place])], sem.at[first + place])
            )
            copies[-1].start()
    diagonal = lax.broadcasted_iota(I32, (128, 128), 0) == lax.broadcasted_iota(I32, (128, 128), 1)
    scale_ref[...] = jnp.concatenate([
        jnp.sum(jnp.where(diagonal, all_peaks[q * 128:(q + 1) * 128, :], 0.0), axis=0, keepdims=True) for q in range(SLOTS // 128)
    ], axis=0).astype(BF16)
    copies.append(pltpu.make_async_copy(scale_ref, scale_out, sem.at[N_ROW]))
    copies[-1].start()
    for copy in copies:
        copy.wait()


def shards(new_rows, old_rows, row_ids, owner):
    vmem = pl.BlockSpec(memory_space=pltpu.VMEM)
    anywhere = pl.BlockSpec(memory_space=pl.ANY)
    places = np.array([PLACE[(number // N_COL, number % N_COL)] * 2 * CAP for number in range(DEVICES)], np.float32)
    places = jnp.asarray(np.repeat(places[:, None], 128, axis=1))
    received = pl.pallas_call(
        kernel,
        out_shape=(
            jax.ShapeDtypeStruct((SLOTS, D), BF16),
            jax.ShapeDtypeStruct((N_COL, SLOTS, SLICE), BF16),
            jax.ShapeDtypeStruct((SLOTS, 128), F32),
            jax.ShapeDtypeStruct((SLICE, SLICE), BF16),
            jax.ShapeDtypeStruct((N_ROW, 1, 128), I32),
        ),
        in_specs=[anywhere] * 5,
        out_specs=(vmem,) * 5,
        scratch_shapes=[
            pltpu.VMEM((ROWS_HERE, SLICE), F32),
            pltpu.VMEM((ROWS_HERE, SLICE), F32),
            pltpu.VMEM((ROWS_HERE // 128, 128), I32),
            pltpu.VMEM((ROWS_HERE // 128, 128), I32),
            pltpu.VMEM((DEVICES, 128), F32),
            pltpu.VMEM((ROWS_HERE, SLICE), BF16),
            pltpu.VMEM((DEVICES, CHUNK, SLICE), BF16),
            pltpu.VMEM((N_ROW, 1, 128), I32),
            pltpu.SemaphoreType.DMA((2 * PAIRS,)),
            pltpu.SemaphoreType.DMA((3,)),
            pltpu.SemaphoreType.REGULAR,
            pltpu.SemaphoreType.REGULAR,
            pltpu.SemaphoreType.REGULAR,
            pltpu.SemaphoreType.DMA,
            pltpu.SemaphoreType.DMA((N_ROW,)),
            pltpu.SemaphoreType.DMA,
            pltpu.SemaphoreType.DMA,
            pltpu.SemaphoreType.DMA,
            pltpu.SemaphoreType.DMA,
        ],
        compiler_params=pltpu.CompilerParams(
            collective_id=0, has_side_effects=True, vmem_limit_bytes=40 * 1024 * 1024
        ),
    )(*(
        pltpu.with_memory_space_constraint(array, pltpu.HBM)
        for array in (new_rows, old_rows, owner.reshape(ROWS_HERE // 128, 128), row_ids.reshape(ROWS_HERE // 128, 128), places)
    ))
    published, scale, ids = pl.pallas_call(
        finish,
        out_shape=(
            jax.ShapeDtypeStruct((SLOTS, D), BF16),
            jax.ShapeDtypeStruct((SLOTS // 128, 128), BF16),
            jax.ShapeDtypeStruct((SLOTS // 128, 128), I32),
        ),
        in_specs=[vmem] * 5,
        out_specs=(anywhere,) * 3,
        scratch_shapes=[
            pltpu.VMEM(((N_ROW - EARLY) * CHUNK, D), BF16),
            pltpu.VMEM((SLOTS, 128), F32),
            pltpu.VMEM((SLOTS // 128, 128), BF16),
            pltpu.VMEM((SLOTS // 128, 128), I32),
            pltpu.SemaphoreType.DMA((N_ROW + 2,)),
        ],
        compiler_params=pltpu.CompilerParams(vmem_limit_bytes=8 * 1024 * 1024),
    )(*(pltpu.with_memory_space_constraint(array, pltpu.VMEM) for array in received))
    return published, scale.reshape(SLOTS), ids.reshape(SLOTS)


def solution(mesh):
    return jax.shard_map(
        shards,
        mesh=mesh,
        in_specs=(P("row", "col"), P("row", "col"), P("row"), P("row", None)),
        out_specs=(P(("row", "col"), None), P(("row", "col")), P(("row", "col"))),
        check_vma=False,
    )
```

```python
import functools
import math
import random

import jax
import jax.numpy as jnp
import numpy as np
from jax import lax
from jax.experimental import pallas as pl
from jax.experimental.pallas import tpu as pltpu
from jax.sharding import PartitionSpec as P

EPSILON = 1e-06
MESH = pl.DeviceIdType.MESH
BF16, F32, I32 = jnp.bfloat16, jnp.float32, jnp.int32

N_ROW, N_COL = 16, 8
DEVICES = N_ROW * N_COL
CAP = 4
BLK = 256
SLICE = 256
D = SLICE * N_COL
ROWS_HERE = BLK * N_COL
CHUNK = CAP * N_COL
SLOTS = CHUNK * N_ROW
PAIRS = N_COL // 2


def parity_signs(size):
    common = lax.broadcasted_iota(I32, (size, size), 0) & lax.broadcasted_iota(I32, (size, size), 1)
    for shift in (4, 2, 1):
        common = common ^ (common >> shift)
    return (1 - 2 * (common & 1)).astype(F32).astype(BF16)


def hops(chunk):
    used = []
    for step in (chunk[0] % 4, chunk[0] // 4, chunk[1] // 2):
        used += [(0, 0), (1, 0), (1, 1), (0, 1)][step]
    return used


def balanced(chunks, seed):
    rest, done, order = list(chunks), [0] * 6, []
    random.Random(seed).shuffle(rest)
    total = [max(1, sum(hops(chunk)[link] for chunk in chunks)) for link in range(6)]
    while rest:
        part = (len(order) + 1) / len(chunks)
        best = min(rest, key=lambda chunk: sum(((d + h) / t - part) ** 2 for d, h, t in zip(done, hops(chunk), total)))
        rest.remove(best)
        order.append(best)
        done = [d + h for d, h in zip(done, hops(best))]
    return order


ALL = [(group, step) for group in range(16) for step in range(8) if group or step]
FIRST = balanced([(group, step) for group in (1, 3, 4, 12) for step in (1, 2, 3, 6, 7)], 5)
LAST = balanced([(group, 0) for group in range(1, 16)], 6)
MIDDLE = balanced([chunk for chunk in ALL if chunk[1] and chunk not in FIRST], 5)
ORDER = FIRST + MIDDLE + LAST
PLACE = {chunk: place for place, chunk in enumerate(ORDER + [(0, 0)])}
SLAB = 64
BATCH = 32


def flip(place, step):
    return (place, place + 1 - 2 * (place % 2), (place + 2) % 4, 3 - place)[step]


def partner_row(row, group):
    return flip(row // 4, group // 4) * 4 + flip(row % 4, group % 4)


def rotate(recv, table, codes, first):
    part = pl.ds(first, SLAB)
    inner = jnp.dot(recv[:, part, :].reshape(N_COL * SLAB, SLICE), table[...], preferred_element_type=F32)
    peaks = []
    for top in range(0, SLAB, CHUNK):
        lines = [inner[c * SLAB + top:c * SLAB + top + CHUNK] for c in range(N_COL)]
        for gap in (1, 2, 4):
            lines = [lines[c] + lines[c + gap] if not c & gap else lines[c - gap] - lines[c] for c in range(N_COL)]
        largest = functools.reduce(jnp.maximum, [jnp.abs(line) for line in lines])
        peaks.append(jnp.max(largest, axis=1, keepdims=True) * (1.0 / math.sqrt(D)))
        factor = (1.0 / math.sqrt(D)) / (peaks[-1] + EPSILON)
        for c in range(N_COL):
            codes[pl.ds(first + top, CHUNK), c * SLICE:(c + 1) * SLICE] = (lines[c] * factor).astype(BF16)
    return peaks


def kernel(
    new_ref, old_ref, owner_hbm, ids_hbm, place_hbm,
    recv, table, ids_recv,
    fresh, stale, owner_ref, ids_ref, place_ref, delta, send, ids_send,
    load_sem, small_sem, x_sem, y_sem, all_sem,
    send_sem, recv_sem, self_sem, ids_send_sem, ids_recv_sem, ids_self_sem,
):
    row = lax.axis_index("row")
    col = lax.axis_index("col")
    y, x = row // 4, row % 4
    z, core = col // 2, col % 2

    def partner(group, step):
        return (partner_row(row, group), flip(z, step // 2) * 2 + (core + step) % 2)

    def loads(pair):
        part = pl.ds(pair * 2 * BLK, 2 * BLK)
        return (
            pltpu.make_async_copy(new_ref.at[part], fresh.at[part], load_sem.at[pair]),
            pltpu.make_async_copy(old_ref.at[part], stale.at[part], load_sem.at[pair + PAIRS]),
        )

    owner_load = pltpu.make_async_copy(owner_hbm, owner_ref, small_sem.at[0])
    ids_load = pltpu.make_async_copy(ids_hbm, ids_ref, small_sem.at[1])
    place_load = pltpu.make_async_copy(place_hbm, place_ref, small_sem.at[2])
    owner_load.start()
    place_load.start()
    for pair in range(PAIRS):
        for copy in loads(pair):
            copy.start()
    ids_load.start()

    barrier = pltpu.get_barrier_semaphore()
    along_x, along_y = (1, 2, 3), (4, 8, 12)

    def tell(sem, groups):
        for group in groups:
            pl.semaphore_signal(sem, inc=1, device_id=partner(group, 0), device_id_type=MESH)

    tell(barrier, along_x + along_y)
    for step in range(1, N_COL):
        pl.semaphore_signal(barrier, inc=1, device_id=partner(0, step), device_id_type=MESH)

    owner_load.wait()
    me = row * N_COL + col
    owner_lines = []
    marks = []
    for block in range(N_COL):
        line = jnp.concatenate([owner_ref[2 * block:2 * block + 1, :], owner_ref[2 * block + 1:2 * block + 2, :]], axis=1) ^ me
        owner_lines.append(line)
        marks.append(jnp.where(lax.broadcasted_iota(I32, (DEVICES, BLK), 0) == line, 1.0, 0.0))
    earlier = jnp.where(
        lax.broadcasted_iota(I32, (BLK, BLK), 0) < lax.broadcasted_iota(I32, (BLK, BLK), 1), 1.0, 0.0
    ).astype(BF16)
    place_load.wait()
    places = jnp.concatenate([place_ref[...]] * (BLK // 128), axis=1)
    slots = []
    keys = []
    for block in range(N_COL):
        counts = jnp.dot(marks[block].astype(BF16), earlier, preferred_element_type=F32)
        slots.append(jnp.sum(marks[block] * counts, axis=0, keepdims=True).astype(I32))
        spot = jnp.sum(marks[block] * (counts + places), axis=0, keepdims=True).astype(I32)
        keys.append(spot + block % 2 * CAP)
    keys = [jnp.concatenate(keys[2 * pair:2 * pair + 2], axis=1) for pair in range(PAIRS)]

    pl.semaphore_wait(barrier, len(along_x + along_y) + N_COL - 1)
    tell(x_sem, along_x)
    tell(y_sem, along_y)
    for pair in range(PAIRS):
        for copy in loads(pair):
            copy.wait()
        part = pl.ds(pair * 2 * BLK, 2 * BLK)
        delta[part, :] = (fresh[part, :] - stale[part, :]).astype(BF16)

    iota = lax.broadcasted_iota(I32, (BATCH * 2 * CAP, 2 * BLK), 0)

    def pack(batch):
        packed = []
        for pair in range(PAIRS):
            picks = jnp.where(iota == keys[pair] - batch * BATCH * 2 * CAP, 1.0, 0.0).astype(BF16)
            rows = jnp.dot(picks, delta[pair * 2 * BLK:(pair + 1) * 2 * BLK, :], preferred_element_type=F32)
            packed.append(rows.reshape(BATCH, 2 * CAP, SLICE))
        for half in range(PAIRS // 2):
            send[batch * BATCH:(batch + 1) * BATCH, half * 16:(half + 1) * 16, :] = jnp.concatenate(
                [packed[2 * half], packed[2 * half + 1]], axis=1
            ).astype(BF16)

    def start(first, end):
        for place in range(first, end):
            group, step = ORDER[place]
            pltpu.make_async_remote_copy(
                src_ref=send.at[place],
                dst_ref=recv.at[col, pl.ds(row * CHUNK, CHUNK)],
                send_sem=send_sem,
                recv_sem=recv_sem.at[group],
                device_id=partner(group, step),
                device_id_type=MESH,
            ).start()

    pack(0)
    pl.semaphore_wait(x_sem, len(along_x))
    tell(all_sem, along_y)
    pl.semaphore_wait(y_sem, len(along_y))
    start(0, len(FIRST))
    pack(1)
    pl.semaphore_wait(all_sem, len(along_y))
    start(len(FIRST), 2 * BATCH)
    pack(2)
    start(2 * BATCH, 3 * BATCH)
    pack(3)
    start(3 * BATCH, DEVICES - 1)
    self_copy = pltpu.make_async_copy(send.at[DEVICES - 1], recv.at[col, pl.ds(row * CHUNK, CHUNK)], self_sem)
    self_copy.start()

    ids_load.wait()
    all_owners = jnp.concatenate(owner_lines, axis=1)
    all_slots = jnp.concatenate(slots, axis=1)
    lane = lax.broadcasted_iota(I32, (1, ROWS_HERE), 1)
    place = (row % 4) * CHUNK + (lane // BLK) * CAP + all_slots
    at_place = jnp.where(lax.broadcasted_iota(I32, (128, ROWS_HERE), 0) == place, 1.0, 0.0).astype(BF16)
    values = jnp.concatenate([ids_ref[i:i + 1, :] for i in range(ROWS_HERE // 128)], axis=1) + 1
    number = lax.broadcasted_iota(I32, (N_ROW, ROWS_HERE), 0)
    mine = all_owners == number * N_COL
    pieces = [jnp.where(mine, part.astype(F32), 0.0).astype(BF16) for part in (values >> 16, (values >> 8) & 255, values & 255)]
    sums = lax.dot_general(
        jnp.concatenate(pieces, axis=0), at_place, (((1,), (1,)), ((), ())), preferred_element_type=F32
    )
    found = (sums[:N_ROW] * 65536.0 + sums[N_ROW:2 * N_ROW] * 256.0 + sums[2 * N_ROW:]).astype(I32)
    for step in range(N_ROW):
        ids_send[step] = found[step:step + 1, :]

    ids_self = pltpu.make_async_copy(ids_send.at[0], ids_recv.at[row], ids_self_sem)
    ids_self.start()

    for group in range(1, N_ROW):
        pltpu.make_async_remote_copy(
            src_ref=ids_send.at[group],
            dst_ref=ids_recv.at[row],
            send_sem=ids_send_sem,
            recv_sem=ids_recv_sem,
            device_id=partner(group, 0),
            device_id_type=MESH,
        ).start()

    table[...] = parity_signs(SLICE)

    def arrived(group):
        chunks = pl.ds(0, N_COL if group else N_COL - 1)
        pltpu.make_async_copy(send.at[chunks], send.at[chunks], recv_sem.at[group]).wait()
        if group == 0:
            self_copy.wait()

    for group in range(N_ROW):
        arrived(group)

    ids_self.wait()
    others = pl.ds(0, N_ROW - 1)
    pltpu.make_async_copy(ids_send.at[others], ids_send.at[others], ids_recv_sem).wait()
    everyone = pl.ds(0, DEVICES - 1)
    pltpu.make_async_copy(send.at[everyone], send.at[everyone], send_sem).wait()
    pltpu.make_async_copy(ids_send.at[others], ids_send.at[others], ids_send_sem).wait()


def finish(recv, table, ids_recv, published, scale_out, ids_out, codes, scale_ref, oid_ref, sem):
    for q in range(SLOTS // 128):
        oid_ref[q:q + 1, :] = ids_recv[4 * q] + ids_recv[4 * q + 1] + ids_recv[4 * q + 2] + ids_recv[4 * q + 3] - 1
    copies = [pltpu.make_async_copy(oid_ref, ids_out, sem.at[0])]
    copies[-1].start()
    peaks = []
    for first in range(0, SLOTS, SLAB):
        peaks += rotate(recv, table, codes, first)
        part = pl.ds(first, SLAB)
        copies.append(pltpu.make_async_copy(codes.at[part], published.at[part], sem.at[2 + first // SLAB]))
        copies[-1].start()
    diagonal = lax.broadcasted_iota(I32, (128, 128), 0) == lax.broadcasted_iota(I32, (128, 128), 1)
    group = 128 // CHUNK
    scale_ref[...] = jnp.concatenate([
        jnp.sum(jnp.where(diagonal, jnp.concatenate(peaks[q * group:(q + 1) * group], axis=0), 0.0), axis=0, keepdims=True)
        for q in range(SLOTS // 128)
    ], axis=0).astype(BF16)
    copies.append(pltpu.make_async_copy(scale_ref, scale_out, sem.at[1]))
    copies[-1].start()
    for copy in copies:
        copy.wait()


def shards(new_rows, old_rows, row_ids, owner):
    vmem = pl.BlockSpec(memory_space=pltpu.VMEM)
    anywhere = pl.BlockSpec(memory_space=pl.ANY)
    places = np.array([PLACE[(number // N_COL, number % N_COL)] * 2 * CAP for number in range(DEVICES)], np.float32)
    places = jnp.asarray(np.repeat(places[:, None], 128, axis=1))
    received = pl.pallas_call(
        kernel,
        out_shape=(
            jax.ShapeDtypeStruct((N_COL, SLOTS, SLICE), BF16),
            jax.ShapeDtypeStruct((SLICE, SLICE), BF16),
            jax.ShapeDtypeStruct((N_ROW, 1, 128), I32),
        ),
        in_specs=[anywhere] * 5,
        out_specs=(vmem,) * 3,
        scratch_shapes=[
            pltpu.VMEM((ROWS_HERE, SLICE), F32),
            pltpu.VMEM((ROWS_HERE, SLICE), F32),
            pltpu.VMEM((ROWS_HERE // 128, 128), I32),
            pltpu.VMEM((ROWS_HERE // 128, 128), I32),
            pltpu.VMEM((DEVICES, 128), F32),
            pltpu.VMEM((ROWS_HERE, SLICE), BF16),
            pltpu.VMEM((DEVICES, CHUNK, SLICE), BF16),
            pltpu.VMEM((N_ROW, 1, 128), I32),
            pltpu.SemaphoreType.DMA((2 * PAIRS,)),
            pltpu.SemaphoreType.DMA((3,)),
            pltpu.SemaphoreType.REGULAR,
            pltpu.SemaphoreType.REGULAR,
            pltpu.SemaphoreType.REGULAR,
            pltpu.SemaphoreType.DMA,
            pltpu.SemaphoreType.DMA((N_ROW,)),
            pltpu.SemaphoreType.DMA,
            pltpu.SemaphoreType.DMA,
            pltpu.SemaphoreType.DMA,
            pltpu.SemaphoreType.DMA,
        ],
        compiler_params=pltpu.CompilerParams(
            collective_id=0, has_side_effects=True, vmem_limit_bytes=40 * 1024 * 1024
        ),
    )(*(
        pltpu.with_memory_space_constraint(array, pltpu.HBM)
        for array in (new_rows, old_rows, owner.reshape(ROWS_HERE // 128, 128), row_ids.reshape(ROWS_HERE // 128, 128), places)
    ))
    published, scale, ids = pl.pallas_call(
        finish,
        out_shape=(
            jax.ShapeDtypeStruct((SLOTS, D), BF16),
            jax.ShapeDtypeStruct((SLOTS // 128, 128), BF16),
            jax.ShapeDtypeStruct((SLOTS // 128, 128), I32),
        ),
        in_specs=[vmem] * 3,
        out_specs=(anywhere,) * 3,
        scratch_shapes=[
            pltpu.VMEM((SLOTS, D), BF16),
            pltpu.VMEM((SLOTS // 128, 128), BF16),
            pltpu.VMEM((SLOTS // 128, 128), I32),
            pltpu.SemaphoreType.DMA((2 + SLOTS // SLAB,)),
        ],
        compiler_params=pltpu.CompilerParams(vmem_limit_bytes=8 * 1024 * 1024),
    )(*(pltpu.with_memory_space_constraint(array, pltpu.VMEM) for array in received))
    return published, scale.reshape(SLOTS), ids.reshape(SLOTS)


def solution(mesh):
    return jax.shard_map(
        shards,
        mesh=mesh,
        in_specs=(P("row", "col"), P("row", "col"), P("row"), P("row", None)),
        out_specs=(P(("row", "col"), None), P(("row", "col")), P(("row", "col"))),
        check_vma=False,
    )
```

```python
import functools
import math
import random

import jax
import jax.numpy as jnp
import numpy as np
from jax import lax
from jax.experimental import pallas as pl
from jax.experimental.pallas import tpu as pltpu
from jax.sharding import PartitionSpec as P

EPSILON = 1e-06
MESH = pl.DeviceIdType.MESH
BF16, F32, I32 = jnp.bfloat16, jnp.float32, jnp.int32

N_ROW, N_COL = 16, 8
DEVICES = N_ROW * N_COL
CAP = 4
BLK = 256
SLICE = 256
D = SLICE * N_COL
ROWS_HERE = BLK * N_COL
CHUNK = CAP * N_COL
SLOTS = CHUNK * N_ROW
PAIRS = N_COL // 2


def parity_signs(size):
    common = lax.broadcasted_iota(I32, (size, size), 0) & lax.broadcasted_iota(I32, (size, size), 1)
    for shift in (4, 2, 1):
        common = common ^ (common >> shift)
    return (1 - 2 * (common & 1)).astype(F32).astype(BF16)


def hops(chunk):
    used = []
    for step in (chunk[0] % 4, chunk[0] // 4, chunk[1] // 2):
        used += [(0, 0), (1, 0), (1, 1), (0, 1)][step]
    return used


def balanced(chunks, seed):
    rest, done, order = list(chunks), [0] * 6, []
    random.Random(seed).shuffle(rest)
    total = [max(1, sum(hops(chunk)[link] for chunk in chunks)) for link in range(6)]
    while rest:
        part = (len(order) + 1) / len(chunks)
        best = min(rest, key=lambda chunk: sum(((d + h) / t - part) ** 2 for d, h, t in zip(done, hops(chunk), total)))
        rest.remove(best)
        order.append(best)
        done = [d + h for d, h in zip(done, hops(best))]
    return order


ALL = [(group, step) for group in range(16) for step in range(8) if group or step]
FIRST = balanced([(group, step) for group in (1, 3, 4, 12) for step in (1, 2, 3, 6, 7)], 5)
LAST = balanced([(group, 0) for group in range(1, 16)], 6)
MIDDLE = balanced([chunk for chunk in ALL if chunk[1] and chunk not in FIRST], 5)
ORDER = FIRST + MIDDLE + LAST
PLACE = {chunk: place for place, chunk in enumerate(ORDER + [(0, 0)])}
SLAB = 32
BATCH = 32


def flip(place, step):
    return (place, place + 1 - 2 * (place % 2), (place + 2) % 4, 3 - place)[step]


def partner_row(row, group):
    return flip(row // 4, group // 4) * 4 + flip(row % 4, group % 4)


def mix(recv, table, first):
    return jnp.dot(
        recv[:, pl.ds(first, SLAB), :].reshape(N_COL * SLAB, SLICE), table[...], preferred_element_type=F32
    )


def rotate(inner, codes, first):
    peaks = []
    for top in range(0, SLAB, CHUNK):
        lines = [inner[c * SLAB + top:c * SLAB + top + CHUNK] for c in range(N_COL)]
        for gap in (1, 2, 4):
            lines = [lines[c] + lines[c + gap] if not c & gap else lines[c - gap] - lines[c] for c in range(N_COL)]
        largest = functools.reduce(jnp.maximum, [jnp.abs(line) for line in lines])
        peaks.append(jnp.max(largest, axis=1, keepdims=True) * (1.0 / math.sqrt(D)))
        factor = (1.0 / math.sqrt(D)) / (peaks[-1] + EPSILON)
        for c in range(N_COL):
            codes[pl.ds(first + top, CHUNK), c * SLICE:(c + 1) * SLICE] = (lines[c] * factor).astype(BF16)
    return peaks


def kernel(
    new_ref, old_ref, owner_hbm, ids_hbm, place_hbm,
    recv, table, ids_recv,
    fresh, stale, owner_ref, ids_ref, place_ref, delta, send, ids_send,
    load_sem, small_sem, x_sem, y_sem, all_sem,
    send_sem, recv_sem, self_sem, ids_send_sem, ids_recv_sem, ids_self_sem,
):
    row = lax.axis_index("row")
    col = lax.axis_index("col")
    y, x = row // 4, row % 4
    z, core = col // 2, col % 2

    def partner(group, step):
        return (partner_row(row, group), flip(z, step // 2) * 2 + (core + step) % 2)

    def loads(pair):
        part = pl.ds(pair * 2 * BLK, 2 * BLK)
        return (
            pltpu.make_async_copy(new_ref.at[part], fresh.at[part], load_sem.at[pair]),
            pltpu.make_async_copy(old_ref.at[part], stale.at[part], load_sem.at[pair + PAIRS]),
        )

    owner_load = pltpu.make_async_copy(owner_hbm, owner_ref, small_sem.at[0])
    ids_load = pltpu.make_async_copy(ids_hbm, ids_ref, small_sem.at[1])
    place_load = pltpu.make_async_copy(place_hbm, place_ref, small_sem.at[2])
    owner_load.start()
    place_load.start()
    for pair in range(PAIRS):
        for copy in loads(pair):
            copy.start()
    ids_load.start()

    barrier = pltpu.get_barrier_semaphore()
    along_x, along_y = (1, 2, 3), (4, 8, 12)

    def tell(sem, groups):
        for group in groups:
            pl.semaphore_signal(sem, inc=1, device_id=partner(group, 0), device_id_type=MESH)

    tell(barrier, along_x + along_y)
    for step in range(1, N_COL):
        pl.semaphore_signal(barrier, inc=1, device_id=partner(0, step), device_id_type=MESH)

    owner_load.wait()
    me = row * N_COL + col
    owner_lines = []
    marks = []
    for block in range(N_COL):
        line = jnp.concatenate([owner_ref[2 * block:2 * block + 1, :], owner_ref[2 * block + 1:2 * block + 2, :]], axis=1) ^ me
        owner_lines.append(line)
        marks.append(jnp.where(lax.broadcasted_iota(I32, (DEVICES, BLK), 0) == line, 1.0, 0.0))
    earlier = jnp.where(
        lax.broadcasted_iota(I32, (BLK, BLK), 0) < lax.broadcasted_iota(I32, (BLK, BLK), 1), 1.0, 0.0
    ).astype(BF16)
    place_load.wait()
    places = jnp.concatenate([place_ref[...]] * (BLK // 128), axis=1)
    slots = []
    keys = []
    for block in range(N_COL):
        counts = jnp.dot(marks[block].astype(BF16), earlier, preferred_element_type=F32)
        slots.append(jnp.sum(marks[block] * counts, axis=0, keepdims=True).astype(I32))
        spot = jnp.sum(marks[block] * (counts + places), axis=0, keepdims=True).astype(I32)
        keys.append(spot + block % 2 * CAP)
    keys = [jnp.concatenate(keys[2 * pair:2 * pair + 2], axis=1) for pair in range(PAIRS)]

    pl.semaphore_wait(barrier, len(along_x + along_y) + N_COL - 1)
    tell(x_sem, along_x)
    tell(y_sem, along_y)
    for pair in range(PAIRS):
        for copy in loads(pair):
            copy.wait()
        part = pl.ds(pair * 2 * BLK, 2 * BLK)
        delta[part, :] = (fresh[part, :] - stale[part, :]).astype(BF16)

    iota = lax.broadcasted_iota(I32, (BATCH * 2 * CAP, 2 * BLK), 0)

    def pack(batch):
        packed = []
        for pair in range(PAIRS):
            picks = jnp.where(iota == keys[pair] - batch * BATCH * 2 * CAP, 1.0, 0.0).astype(BF16)
            rows = jnp.dot(picks, delta[pair * 2 * BLK:(pair + 1) * 2 * BLK, :], preferred_element_type=F32)
            packed.append(rows.reshape(BATCH, 2 * CAP, SLICE))
        for half in range(PAIRS // 2):
            send[batch * BATCH:(batch + 1) * BATCH, half * 16:(half + 1) * 16, :] = jnp.concatenate(
                [packed[2 * half], packed[2 * half + 1]], axis=1
            ).astype(BF16)

    def start(first, end):
        for place in range(first, end):
            group, step = ORDER[place]
            pltpu.make_async_remote_copy(
                src_ref=send.at[place],
                dst_ref=recv.at[col, pl.ds(row * CHUNK, CHUNK)],
                send_sem=send_sem,
                recv_sem=recv_sem.at[group],
                device_id=partner(group, step),
                device_id_type=MESH,
            ).start()

    pack(0)
    pl.semaphore_wait(x_sem, len(along_x))
    tell(all_sem, along_y)
    pl.semaphore_wait(y_sem, len(along_y))
    start(0, len(FIRST))
    pack(1)
    pl.semaphore_wait(all_sem, len(along_y))
    start(len(FIRST), 2 * BATCH)
    pack(2)
    start(2 * BATCH, 3 * BATCH)
    pack(3)
    start(3 * BATCH, DEVICES - 1)
    self_copy = pltpu.make_async_copy(send.at[DEVICES - 1], recv.at[col, pl.ds(row * CHUNK, CHUNK)], self_sem)
    self_copy.start()

    ids_load.wait()
    all_owners = jnp.concatenate(owner_lines, axis=1)
    all_slots = jnp.concatenate(slots, axis=1)
    lane = lax.broadcasted_iota(I32, (1, ROWS_HERE), 1)
    place = (row % 4) * CHUNK + (lane // BLK) * CAP + all_slots
    at_place = jnp.where(lax.broadcasted_iota(I32, (128, ROWS_HERE), 0) == place, 1.0, 0.0).astype(BF16)
    values = jnp.concatenate([ids_ref[i:i + 1, :] for i in range(ROWS_HERE // 128)], axis=1) + 1
    number = lax.broadcasted_iota(I32, (N_ROW, ROWS_HERE), 0)
    mine = all_owners == number * N_COL
    pieces = [jnp.where(mine, part.astype(F32), 0.0).astype(BF16) for part in (values >> 16, (values >> 8) & 255, values & 255)]
    sums = lax.dot_general(
        jnp.concatenate(pieces, axis=0), at_place, (((1,), (1,)), ((), ())), preferred_element_type=F32
    )
    found = (sums[:N_ROW] * 65536.0 + sums[N_ROW:2 * N_ROW] * 256.0 + sums[2 * N_ROW:]).astype(I32)
    for step in range(N_ROW):
        ids_send[step] = found[step:step + 1, :]

    ids_self = pltpu.make_async_copy(ids_send.at[0], ids_recv.at[row], ids_self_sem)
    ids_self.start()

    for group in range(1, N_ROW):
        pltpu.make_async_remote_copy(
            src_ref=ids_send.at[group],
            dst_ref=ids_recv.at[row],
            send_sem=ids_send_sem,
            recv_sem=ids_recv_sem,
            device_id=partner(group, 0),
            device_id_type=MESH,
        ).start()

    table[...] = parity_signs(SLICE)

    def arrived(group):
        chunks = pl.ds(0, N_COL if group else N_COL - 1)
        pltpu.make_async_copy(send.at[chunks], send.at[chunks], recv_sem.at[group]).wait()
        if group == 0:
            self_copy.wait()

    for group in range(N_ROW):
        arrived(group)

    ids_self.wait()
    others = pl.ds(0, N_ROW - 1)
    pltpu.make_async_copy(ids_send.at[others], ids_send.at[others], ids_recv_sem).wait()
    everyone = pl.ds(0, DEVICES - 1)
    pltpu.make_async_copy(send.at[everyone], send.at[everyone], send_sem).wait()
    pltpu.make_async_copy(ids_send.at[others], ids_send.at[others], ids_send_sem).wait()


def finish(recv, table, ids_recv, published, scale_out, ids_out, codes, scale_ref, oid_ref, sem):
    for q in range(SLOTS // 128):
        oid_ref[q:q + 1, :] = ids_recv[4 * q] + ids_recv[4 * q + 1] + ids_recv[4 * q + 2] + ids_recv[4 * q + 3] - 1
    copies = [pltpu.make_async_copy(oid_ref, ids_out, sem.at[0])]
    copies[-1].start()
    peaks = []
    following = mix(recv, table, 0)
    for first in range(0, SLOTS, SLAB):
        inner = following
        if first + SLAB < SLOTS:
            following = mix(recv, table, first + SLAB)
        peaks += rotate(inner, codes, first)
        part = pl.ds(first, SLAB)
        copies.append(pltpu.make_async_copy(codes.at[part], published.at[part], sem.at[2 + first // SLAB]))
        copies[-1].start()
    diagonal = lax.broadcasted_iota(I32, (128, 128), 0) == lax.broadcasted_iota(I32, (128, 128), 1)
    group = 128 // CHUNK
    scale_ref[...] = jnp.concatenate([
        jnp.sum(jnp.where(diagonal, jnp.concatenate(peaks[q * group:(q + 1) * group], axis=0), 0.0), axis=0, keepdims=True)
        for q in range(SLOTS // 128)
    ], axis=0).astype(BF16)
    copies.append(pltpu.make_async_copy(scale_ref, scale_out, sem.at[1]))
    copies[-1].start()
    for copy in copies:
        copy.wait()


def shards(new_rows, old_rows, row_ids, owner):
    vmem = pl.BlockSpec(memory_space=pltpu.VMEM)
    anywhere = pl.BlockSpec(memory_space=pl.ANY)
    places = np.array([PLACE[(number // N_COL, number % N_COL)] * 2 * CAP for number in range(DEVICES)], np.float32)
    places = jnp.asarray(np.repeat(places[:, None], 128, axis=1))
    received = pl.pallas_call(
        kernel,
        out_shape=(
            jax.ShapeDtypeStruct((N_COL, SLOTS, SLICE), BF16),
            jax.ShapeDtypeStruct((SLICE, SLICE), BF16),
            jax.ShapeDtypeStruct((N_ROW, 1, 128), I32),
        ),
        in_specs=[anywhere] * 5,
        out_specs=(vmem,) * 3,
        scratch_shapes=[
            pltpu.VMEM((ROWS_HERE, SLICE), F32),
            pltpu.VMEM((ROWS_HERE, SLICE), F32),
            pltpu.VMEM((ROWS_HERE // 128, 128), I32),
            pltpu.VMEM((ROWS_HERE // 128, 128), I32),
            pltpu.VMEM((DEVICES, 128), F32),
            pltpu.VMEM((ROWS_HERE, SLICE), BF16),
            pltpu.VMEM((DEVICES, CHUNK, SLICE), BF16),
            pltpu.VMEM((N_ROW, 1, 128), I32),
            pltpu.SemaphoreType.DMA((2 * PAIRS,)),
            pltpu.SemaphoreType.DMA((3,)),
            pltpu.SemaphoreType.REGULAR,
            pltpu.SemaphoreType.REGULAR,
            pltpu.SemaphoreType.REGULAR,
            pltpu.SemaphoreType.DMA,
            pltpu.SemaphoreType.DMA((N_ROW,)),
            pltpu.SemaphoreType.DMA,
            pltpu.SemaphoreType.DMA,
            pltpu.SemaphoreType.DMA,
            pltpu.SemaphoreType.DMA,
        ],
        compiler_params=pltpu.CompilerParams(
            collective_id=0, has_side_effects=True, vmem_limit_bytes=40 * 1024 * 1024
        ),
    )(*(
        pltpu.with_memory_space_constraint(array, pltpu.HBM)
        for array in (new_rows, old_rows, owner.reshape(ROWS_HERE // 128, 128), row_ids.reshape(ROWS_HERE // 128, 128), places)
    ))
    published, scale, ids = pl.pallas_call(
        finish,
        out_shape=(
            jax.ShapeDtypeStruct((SLOTS, D), BF16),
            jax.ShapeDtypeStruct((SLOTS // 128, 128), BF16),
            jax.ShapeDtypeStruct((SLOTS // 128, 128), I32),
        ),
        in_specs=[vmem] * 3,
        out_specs=(anywhere,) * 3,
        scratch_shapes=[
            pltpu.VMEM((SLOTS, D), BF16),
            pltpu.VMEM((SLOTS // 128, 128), BF16),
            pltpu.VMEM((SLOTS // 128, 128), I32),
            pltpu.SemaphoreType.DMA((2 + SLOTS // SLAB,)),
        ],
        compiler_params=pltpu.CompilerParams(vmem_limit_bytes=8 * 1024 * 1024),
    )(*(pltpu.with_memory_space_constraint(array, pltpu.VMEM) for array in received))
    return published, scale.reshape(SLOTS), ids.reshape(SLOTS)


def solution(mesh):
    return jax.shard_map(
        shards,
        mesh=mesh,
        in_specs=(P("row", "col"), P("row", "col"), P("row"), P("row", None)),
        out_specs=(P(("row", "col"), None), P(("row", "col")), P(("row", "col"))),
        check_vma=False,
    )
```

```python
import functools
import math
import random

import jax
import jax.numpy as jnp
import numpy as np
from jax import lax
from jax.experimental import pallas as pl
from jax.experimental.pallas import tpu as pltpu
from jax.sharding import PartitionSpec as P

EPSILON = 1e-06
MESH = pl.DeviceIdType.MESH
BF16, F32, I32 = jnp.bfloat16, jnp.float32, jnp.int32

N_ROW, N_COL = 16, 8
DEVICES = N_ROW * N_COL
CAP = 4
BLK = 256
SLICE = 256
D = SLICE * N_COL
ROWS_HERE = BLK * N_COL
CHUNK = CAP * N_COL
SLOTS = CHUNK * N_ROW
PAIRS = N_COL // 2


def parity_signs(size):
    common = lax.broadcasted_iota(I32, (size, size), 0) & lax.broadcasted_iota(I32, (size, size), 1)
    for shift in (4, 2, 1):
        common = common ^ (common >> shift)
    return (1 - 2 * (common & 1)).astype(F32).astype(BF16)


def hops(chunk):
    used = []
    for step in (chunk[0] % 4, chunk[0] // 4, chunk[1] // 2):
        used += [(0, 0), (1, 0), (1, 1), (0, 1)][step]
    return used


def balanced(chunks, seed):
    rest, done, order = list(chunks), [0] * 6, []
    random.Random(seed).shuffle(rest)
    total = [max(1, sum(hops(chunk)[link] for chunk in chunks)) for link in range(6)]
    while rest:
        part = (len(order) + 1) / len(chunks)
        best = min(rest, key=lambda chunk: sum(((d + h) / t - part) ** 2 for d, h, t in zip(done, hops(chunk), total)))
        rest.remove(best)
        order.append(best)
        done = [d + h for d, h in zip(done, hops(best))]
    return order


ALL = [(group, step) for group in range(16) for step in range(8) if group or step]
FIRST = balanced([(group, step) for group in (1, 3, 4, 12) for step in (1, 2, 3, 6, 7)], 5)
LAST = balanced([(group, 0) for group in range(1, 16)], 6)
MIDDLE = balanced([chunk for chunk in ALL if chunk[1] and chunk not in FIRST], 5)
ORDER = FIRST + MIDDLE + LAST
PLACE = {chunk: place for place, chunk in enumerate(ORDER + [(0, 0)])}
SLAB = 32
BATCH = 32


def flip(place, step):
    return (place, place + 1 - 2 * (place % 2), (place + 2) % 4, 3 - place)[step]


def partner_row(row, group):
    return flip(row // 4, group // 4) * 4 + flip(row % 4, group % 4)


def mix(recv, table, first):
    return jnp.dot(
        recv[:, pl.ds(first, SLAB), :].reshape(N_COL * SLAB, SLICE), table[...], preferred_element_type=F32
    )


def rotate(inner, codes, first):
    peaks = []
    for top in range(0, SLAB, CHUNK):
        lines = [inner[c * SLAB + top:c * SLAB + top + CHUNK] for c in range(N_COL)]
        for gap in (1, 2, 4):
            lines = [lines[c] + lines[c + gap] if not c & gap else lines[c - gap] - lines[c] for c in range(N_COL)]
        largest = functools.reduce(jnp.maximum, [jnp.abs(line) for line in lines])
        peaks.append(jnp.max(largest, axis=1, keepdims=True) * (1.0 / math.sqrt(D)))
        factor = (1.0 / math.sqrt(D)) / (peaks[-1] + EPSILON)
        for c in range(N_COL):
            codes[pl.ds(first + top, CHUNK), c * SLICE:(c + 1) * SLICE] = (lines[c] * factor).astype(BF16)
    return peaks


def kernel(
    new_ref, old_ref, owner_hbm, ids_hbm, place_hbm,
    recv, table, ids_recv,
    fresh, stale, owner_ref, ids_ref, place_ref, delta, send, ids_send,
    load_sem, small_sem, x_sem, y_sem, all_sem,
    send_sem, recv_sem, self_sem, ids_send_sem, ids_recv_sem, ids_self_sem,
):
    row = lax.axis_index("row")
    col = lax.axis_index("col")
    y, x = row // 4, row % 4
    z, core = col // 2, col % 2

    def partner(group, step):
        return (partner_row(row, group), flip(z, step // 2) * 2 + (core + step) % 2)

    def loads(pair):
        part = pl.ds(pair * 2 * BLK, 2 * BLK)
        return (
            pltpu.make_async_copy(new_ref.at[part], fresh.at[part], load_sem.at[pair]),
            pltpu.make_async_copy(old_ref.at[part], stale.at[part], load_sem.at[pair + PAIRS]),
        )

    owner_load = pltpu.make_async_copy(owner_hbm, owner_ref, small_sem.at[0])
    ids_load = pltpu.make_async_copy(ids_hbm, ids_ref, small_sem.at[1])
    place_load = pltpu.make_async_copy(place_hbm, place_ref, small_sem.at[2])
    owner_load.start()
    place_load.start()
    for pair in range(PAIRS):
        for copy in loads(pair):
            copy.start()
    ids_load.start()

    barrier = pltpu.get_barrier_semaphore()
    along_x, along_y = (1, 2, 3), (4, 8, 12)

    def tell(sem, groups):
        for group in groups:
            pl.semaphore_signal(sem, inc=1, device_id=partner(group, 0), device_id_type=MESH)

    tell(barrier, along_x + along_y)
    for step in range(1, N_COL):
        pl.semaphore_signal(barrier, inc=1, device_id=partner(0, step), device_id_type=MESH)

    owner_load.wait()
    me = row * N_COL + col
    owner_lines = []
    marks = []
    for block in range(N_COL):
        line = jnp.concatenate([owner_ref[2 * block:2 * block + 1, :], owner_ref[2 * block + 1:2 * block + 2, :]], axis=1) ^ me
        owner_lines.append(line)
        marks.append(jnp.where(lax.broadcasted_iota(I32, (DEVICES, BLK), 0) == line, 1.0, 0.0))
    earlier = jnp.where(
        lax.broadcasted_iota(I32, (BLK, BLK), 0) < lax.broadcasted_iota(I32, (BLK, BLK), 1), 1.0, 0.0
    ).astype(BF16)
    place_load.wait()
    places = jnp.concatenate([place_ref[...]] * (BLK // 128), axis=1)
    slots = []
    keys = []
    for block in range(N_COL):
        counts = jnp.dot(marks[block].astype(BF16), earlier, preferred_element_type=F32)
        slots.append(jnp.sum(marks[block] * counts, axis=0, keepdims=True).astype(I32))
        spot = jnp.sum(marks[block] * (counts + places), axis=0, keepdims=True).astype(I32)
        keys.append(spot + block % 2 * CAP)
    keys = [jnp.concatenate(keys[2 * pair:2 * pair + 2], axis=1) for pair in range(PAIRS)]

    pl.semaphore_wait(barrier, len(along_x + along_y) + N_COL - 1)
    tell(x_sem, along_x)
    tell(y_sem, along_y)
    for pair in range(PAIRS):
        for copy in loads(pair):
            copy.wait()
        part = pl.ds(pair * 2 * BLK, 2 * BLK)
        delta[part, :] = (fresh[part, :] - stale[part, :]).astype(BF16)

    iota = lax.broadcasted_iota(I32, (BATCH * 2 * CAP, 2 * BLK), 0)

    def pack(batch):
        packed = []
        for pair in range(PAIRS):
            picks = jnp.where(iota == keys[pair] - batch * BATCH * 2 * CAP, 1.0, 0.0).astype(BF16)
            rows = jnp.dot(picks, delta[pair * 2 * BLK:(pair + 1) * 2 * BLK, :], preferred_element_type=F32)
            packed.append(rows.reshape(BATCH, 2 * CAP, SLICE))
        for half in range(PAIRS // 2):
            send[batch * BATCH:(batch + 1) * BATCH, half * 16:(half + 1) * 16, :] = jnp.concatenate(
                [packed[2 * half], packed[2 * half + 1]], axis=1
            ).astype(BF16)

    def start(first, end):
        for place in range(first, end):
            group, step = ORDER[place]
            pltpu.make_async_remote_copy(
                src_ref=send.at[place],
                dst_ref=recv.at[col, pl.ds(row * CHUNK, CHUNK)],
                send_sem=send_sem,
                recv_sem=recv_sem.at[group],
                device_id=partner(group, step),
                device_id_type=MESH,
            ).start()

    pack(0)
    pl.semaphore_wait(x_sem, len(along_x))
    tell(all_sem, along_y)
    pl.semaphore_wait(y_sem, len(along_y))
    start(0, len(FIRST))
    pack(1)
    pl.semaphore_wait(all_sem, len(along_y))
    start(len(FIRST), 2 * BATCH)
    pack(2)
    start(2 * BATCH, 3 * BATCH)
    ids_load.wait()
    all_owners = jnp.concatenate(owner_lines, axis=1)
    all_slots = jnp.concatenate(slots, axis=1)
    lane = lax.broadcasted_iota(I32, (1, ROWS_HERE), 1)
    place = (row % 4) * CHUNK + (lane // BLK) * CAP + all_slots
    at_place = jnp.where(lax.broadcasted_iota(I32, (128, ROWS_HERE), 0) == place, 1.0, 0.0).astype(BF16)
    values = jnp.concatenate([ids_ref[i:i + 1, :] for i in range(ROWS_HERE // 128)], axis=1) + 1
    number = lax.broadcasted_iota(I32, (N_ROW, ROWS_HERE), 0)
    mine = all_owners == number * N_COL
    pieces = [jnp.where(mine, part.astype(F32), 0.0).astype(BF16) for part in (values >> 16, (values >> 8) & 255, values & 255)]
    sums = lax.dot_general(
        jnp.concatenate(pieces, axis=0), at_place, (((1,), (1,)), ((), ())), preferred_element_type=F32
    )
    found = (sums[:N_ROW] * 65536.0 + sums[N_ROW:2 * N_ROW] * 256.0 + sums[2 * N_ROW:]).astype(I32)
    for step in range(N_ROW):
        ids_send[step] = found[step:step + 1, :]

    ids_self = pltpu.make_async_copy(ids_send.at[0], ids_recv.at[row], ids_self_sem)
    ids_self.start()

    for group in range(1, N_ROW):
        pltpu.make_async_remote_copy(
            src_ref=ids_send.at[group],
            dst_ref=ids_recv.at[row],
            send_sem=ids_send_sem,
            recv_sem=ids_recv_sem,
            device_id=partner(group, 0),
            device_id_type=MESH,
        ).start()

    pack(3)
    start(3 * BATCH, DEVICES - 1)
    self_copy = pltpu.make_async_copy(send.at[DEVICES - 1], recv.at[col, pl.ds(row * CHUNK, CHUNK)], self_sem)
    self_copy.start()

    table[...] = parity_signs(SLICE)

    def arrived(group):
        chunks = pl.ds(0, N_COL if group else N_COL - 1)
        pltpu.make_async_copy(send.at[chunks], send.at[chunks], recv_sem.at[group]).wait()
        if group == 0:
            self_copy.wait()

    for group in range(N_ROW):
        arrived(group)

    ids_self.wait()
    others = pl.ds(0, N_ROW - 1)
    pltpu.make_async_copy(ids_send.at[others], ids_send.at[others], ids_recv_sem).wait()
    everyone = pl.ds(0, DEVICES - 1)
    pltpu.make_async_copy(send.at[everyone], send.at[everyone], send_sem).wait()
    pltpu.make_async_copy(ids_send.at[others], ids_send.at[others], ids_send_sem).wait()


def finish(recv, table, ids_recv, published, scale_out, ids_out, codes, scale_ref, oid_ref, sem):
    for q in range(SLOTS // 128):
        oid_ref[q:q + 1, :] = ids_recv[4 * q] + ids_recv[4 * q + 1] + ids_recv[4 * q + 2] + ids_recv[4 * q + 3] - 1
    copies = [pltpu.make_async_copy(oid_ref, ids_out, sem.at[0])]
    copies[-1].start()
    peaks = []
    following = mix(recv, table, 0)
    for first in range(0, SLOTS, SLAB):
        inner = following
        if first + SLAB < SLOTS:
            following = mix(recv, table, first + SLAB)
        peaks += rotate(inner, codes, first)
        part = pl.ds(first, SLAB)
        copies.append(pltpu.make_async_copy(codes.at[part], published.at[part], sem.at[2 + first // SLAB]))
        copies[-1].start()
    diagonal = lax.broadcasted_iota(I32, (128, 128), 0) == lax.broadcasted_iota(I32, (128, 128), 1)
    group = 128 // CHUNK
    scale_ref[...] = jnp.concatenate([
        jnp.sum(jnp.where(diagonal, jnp.concatenate(peaks[q * group:(q + 1) * group], axis=0), 0.0), axis=0, keepdims=True)
        for q in range(SLOTS // 128)
    ], axis=0).astype(BF16)
    copies.append(pltpu.make_async_copy(scale_ref, scale_out, sem.at[1]))
    copies[-1].start()
    for copy in copies:
        copy.wait()


def shards(new_rows, old_rows, row_ids, owner):
    vmem = pl.BlockSpec(memory_space=pltpu.VMEM)
    anywhere = pl.BlockSpec(memory_space=pl.ANY)
    places = np.array([PLACE[(number // N_COL, number % N_COL)] * 2 * CAP for number in range(DEVICES)], np.float32)
    places = jnp.asarray(np.repeat(places[:, None], 128, axis=1))
    received = pl.pallas_call(
        kernel,
        out_shape=(
            jax.ShapeDtypeStruct((N_COL, SLOTS, SLICE), BF16),
            jax.ShapeDtypeStruct((SLICE, SLICE), BF16),
            jax.ShapeDtypeStruct((N_ROW, 1, 128), I32),
        ),
        in_specs=[anywhere] * 5,
        out_specs=(vmem,) * 3,
        scratch_shapes=[
            pltpu.VMEM((ROWS_HERE, SLICE), F32),
            pltpu.VMEM((ROWS_HERE, SLICE), F32),
            pltpu.VMEM((ROWS_HERE // 128, 128), I32),
            pltpu.VMEM((ROWS_HERE // 128, 128), I32),
            pltpu.VMEM((DEVICES, 128), F32),
            pltpu.VMEM((ROWS_HERE, SLICE), BF16),
            pltpu.VMEM((DEVICES, CHUNK, SLICE), BF16),
            pltpu.VMEM((N_ROW, 1, 128), I32),
            pltpu.SemaphoreType.DMA((2 * PAIRS,)),
            pltpu.SemaphoreType.DMA((3,)),
            pltpu.SemaphoreType.REGULAR,
            pltpu.SemaphoreType.REGULAR,
            pltpu.SemaphoreType.REGULAR,
            pltpu.SemaphoreType.DMA,
            pltpu.SemaphoreType.DMA((N_ROW,)),
            pltpu.SemaphoreType.DMA,
            pltpu.SemaphoreType.DMA,
            pltpu.SemaphoreType.DMA,
            pltpu.SemaphoreType.DMA,
        ],
        compiler_params=pltpu.CompilerParams(
            collective_id=0, has_side_effects=True, vmem_limit_bytes=40 * 1024 * 1024
        ),
    )(*(
        pltpu.with_memory_space_constraint(array, pltpu.HBM)
        for array in (new_rows, old_rows, owner.reshape(ROWS_HERE // 128, 128), row_ids.reshape(ROWS_HERE // 128, 128), places)
    ))
    published, scale, ids = pl.pallas_call(
        finish,
        out_shape=(
            jax.ShapeDtypeStruct((SLOTS, D), BF16),
            jax.ShapeDtypeStruct((SLOTS // 128, 128), BF16),
            jax.ShapeDtypeStruct((SLOTS // 128, 128), I32),
        ),
        in_specs=[vmem] * 3,
        out_specs=(anywhere,) * 3,
        scratch_shapes=[
            pltpu.VMEM((SLOTS, D), BF16),
            pltpu.VMEM((SLOTS // 128, 128), BF16),
            pltpu.VMEM((SLOTS // 128, 128), I32),
            pltpu.SemaphoreType.DMA((2 + SLOTS // SLAB,)),
        ],
        compiler_params=pltpu.CompilerParams(vmem_limit_bytes=8 * 1024 * 1024),
    )(*(pltpu.with_memory_space_constraint(array, pltpu.VMEM) for array in received))
    return published, scale.reshape(SLOTS), ids.reshape(SLOTS)


def solution(mesh):
    return jax.shard_map(
        shards,
        mesh=mesh,
        in_specs=(P("row", "col"), P("row", "col"), P("row"), P("row", None)),
        out_specs=(P(("row", "col"), None), P(("row", "col")), P(("row", "col"))),
        check_vma=False,
    )
```

```python
import functools
import math
import random

import jax
import jax.numpy as jnp
import numpy as np
from jax import lax
from jax.experimental import pallas as pl
from jax.experimental.pallas import tpu as pltpu
from jax.sharding import PartitionSpec as P

EPSILON = 1e-06
MESH = pl.DeviceIdType.MESH
BF16, F32, I32 = jnp.bfloat16, jnp.float32, jnp.int32

N_ROW, N_COL = 16, 8
DEVICES = N_ROW * N_COL
CAP = 4
BLK = 256
SLICE = 256
D = SLICE * N_COL
ROWS_HERE = BLK * N_COL
CHUNK = CAP * N_COL
SLOTS = CHUNK * N_ROW
PAIRS = N_COL // 2


def parity_signs(size):
    common = lax.broadcasted_iota(I32, (size, size), 0) & lax.broadcasted_iota(I32, (size, size), 1)
    for shift in (4, 2, 1):
        common = common ^ (common >> shift)
    return (1 - 2 * (common & 1)).astype(F32).astype(BF16)


def hops(chunk):
    used = []
    for step in (chunk[0] % 4, chunk[0] // 4, chunk[1] // 2):
        used += [(0, 0), (1, 0), (1, 1), (0, 1)][step]
    return used


def balanced(chunks, seed):
    rest, done, order = list(chunks), [0] * 6, []
    random.Random(seed).shuffle(rest)
    total = [max(1, sum(hops(chunk)[link] for chunk in chunks)) for link in range(6)]
    while rest:
        part = (len(order) + 1) / len(chunks)
        best = min(rest, key=lambda chunk: sum(((d + h) / t - part) ** 2 for d, h, t in zip(done, hops(chunk), total)))
        rest.remove(best)
        order.append(best)
        done = [d + h for d, h in zip(done, hops(best))]
    return order


ALL = [(group, step) for group in range(16) for step in range(8) if group or step]
FIRST = balanced([(group, step) for group in (1, 3, 4, 12) for step in (1, 2, 3, 6, 7)], 5)
LAST = balanced([(group, 0) for group in range(1, 16)], 6)
MIDDLE = balanced([chunk for chunk in ALL if chunk[1] and chunk not in FIRST], 5)
ORDER = FIRST + MIDDLE + LAST
PLACE = {chunk: place for place, chunk in enumerate(ORDER + [(0, 0)])}
SLAB = 32
BATCH = 32


def flip(place, step):
    return (place, place + 1 - 2 * (place % 2), (place + 2) % 4, 3 - place)[step]


def partner_row(row, group):
    return flip(row // 4, group // 4) * 4 + flip(row % 4, group % 4)


def mix(recv, table, first):
    return jnp.dot(
        recv[:, pl.ds(first, SLAB), :].reshape(N_COL * SLAB, SLICE), table[...], preferred_element_type=F32
    )


def rotate(inner, codes, first):
    peaks = []
    for top in range(0, SLAB, CHUNK):
        lines = [inner[c * SLAB + top:c * SLAB + top + CHUNK] for c in range(N_COL)]
        for gap in (1, 2, 4):
            lines = [lines[c] + lines[c + gap] if not c & gap else lines[c - gap] - lines[c] for c in range(N_COL)]
        largest = functools.reduce(jnp.maximum, [jnp.abs(line) for line in lines])
        peaks.append(jnp.max(largest, axis=1, keepdims=True) * (1.0 / math.sqrt(D)))
        factor = (1.0 / math.sqrt(D)) / (peaks[-1] + EPSILON)
        for c in range(N_COL):
            codes[pl.ds(first + top, CHUNK), c * SLICE:(c + 1) * SLICE] = (lines[c] * factor).astype(BF16)
    return peaks


def kernel(
    new_ref, old_ref, owner_hbm, ids_hbm, place_hbm,
    recv, table, ids_recv,
    fresh, stale, owner_ref, ids_ref, place_ref, delta, send, ids_send,
    load_sem, small_sem, x_sem, y_sem, all_sem,
    send_sem, recv_sem, self_sem, ids_send_sem, ids_recv_sem, ids_self_sem,
):
    row = lax.axis_index("row")
    col = lax.axis_index("col")
    y, x = row // 4, row % 4
    z, core = col // 2, col % 2

    def partner(group, step):
        return (partner_row(row, group), flip(z, step // 2) * 2 + (core + step) % 2)

    def loads(pair):
        part = pl.ds(pair * 2 * BLK, 2 * BLK)
        return (
            pltpu.make_async_copy(new_ref.at[part], fresh.at[part], load_sem.at[pair]),
            pltpu.make_async_copy(old_ref.at[part], stale.at[part], load_sem.at[pair + PAIRS]),
        )

    owner_load = pltpu.make_async_copy(owner_hbm, owner_ref, small_sem.at[0])
    ids_load = pltpu.make_async_copy(ids_hbm, ids_ref, small_sem.at[1])
    place_load = pltpu.make_async_copy(place_hbm, place_ref, small_sem.at[2])
    owner_load.start()
    place_load.start()
    for pair in range(PAIRS):
        for copy in loads(pair):
            copy.start()
    ids_load.start()

    barrier = pltpu.get_barrier_semaphore()
    along_x, along_y = (1, 2, 3), (4, 8, 12)

    def tell(sem, groups):
        for group in groups:
            pl.semaphore_signal(sem, inc=1, device_id=partner(group, 0), device_id_type=MESH)

    tell(barrier, along_x + along_y)
    for step in range(1, N_COL):
        pl.semaphore_signal(barrier, inc=1, device_id=partner(0, step), device_id_type=MESH)

    owner_load.wait()
    me = row * N_COL + col
    owner_lines = []
    marks = []
    for block in range(N_COL):
        line = jnp.concatenate([owner_ref[2 * block:2 * block + 1, :], owner_ref[2 * block + 1:2 * block + 2, :]], axis=1) ^ me
        owner_lines.append(line)
        marks.append(jnp.where(lax.broadcasted_iota(I32, (DEVICES, BLK), 0) == line, 1.0, 0.0))
    earlier = jnp.where(
        lax.broadcasted_iota(I32, (BLK, BLK), 0) < lax.broadcasted_iota(I32, (BLK, BLK), 1), 1.0, 0.0
    ).astype(BF16)
    place_load.wait()
    places = jnp.concatenate([place_ref[...]] * (BLK // 128), axis=1)
    slots = []
    keys = []
    for block in range(N_COL):
        counts = jnp.dot(marks[block].astype(BF16), earlier, preferred_element_type=F32)
        slots.append(jnp.sum(marks[block] * counts, axis=0, keepdims=True).astype(I32))
        spot = jnp.sum(marks[block] * (counts + places), axis=0, keepdims=True).astype(I32)
        keys.append(spot + block % 2 * CAP)
    keys = [jnp.concatenate(keys[2 * pair:2 * pair + 2], axis=1) for pair in range(PAIRS)]

    pl.semaphore_wait(barrier, len(along_x + along_y) + N_COL - 1)
    tell(x_sem, along_x)
    tell(y_sem, along_y)
    for pair in range(PAIRS):
        for copy in loads(pair):
            copy.wait()
        part = pl.ds(pair * 2 * BLK, 2 * BLK)
        delta[part, :] = (fresh[part, :] - stale[part, :]).astype(BF16)

    iota = lax.broadcasted_iota(I32, (BATCH * 2 * CAP, 2 * BLK), 0)

    def pack(batch):
        packed = []
        for pair in range(PAIRS):
            picks = jnp.where(iota == keys[pair] - batch * BATCH * 2 * CAP, 1.0, 0.0).astype(BF16)
            rows = jnp.dot(picks, delta[pair * 2 * BLK:(pair + 1) * 2 * BLK, :], preferred_element_type=F32)
            packed.append(rows.reshape(BATCH, 2 * CAP, SLICE))
        for half in range(PAIRS // 2):
            send[batch * BATCH:(batch + 1) * BATCH, half * 16:(half + 1) * 16, :] = jnp.concatenate(
                [packed[2 * half], packed[2 * half + 1]], axis=1
            ).astype(BF16)

    def start(first, end):
        for place in range(first, end):
            group, step = ORDER[place]
            pltpu.make_async_remote_copy(
                src_ref=send.at[place],
                dst_ref=recv.at[col, pl.ds(row * CHUNK, CHUNK)],
                send_sem=send_sem,
                recv_sem=recv_sem.at[group],
                device_id=partner(group, step),
                device_id_type=MESH,
            ).start()

    pack(0)
    pl.semaphore_wait(x_sem, len(along_x))
    tell(all_sem, along_y)
    pl.semaphore_wait(y_sem, len(along_y))
    start(0, len(FIRST))
    pack(1)
    pl.semaphore_wait(all_sem, len(along_y))
    start(len(FIRST), 2 * BATCH)
    pack(2)
    start(2 * BATCH, 3 * BATCH)
    ids_load.wait()
    all_owners = jnp.concatenate(owner_lines, axis=1)
    all_slots = jnp.concatenate(slots, axis=1)
    lane = lax.broadcasted_iota(I32, (1, ROWS_HERE), 1)
    place = (row % 4) * CHUNK + (lane // BLK) * CAP + all_slots
    at_place = jnp.where(lax.broadcasted_iota(I32, (128, ROWS_HERE), 0) == place, 1.0, 0.0).astype(BF16)
    values = jnp.concatenate([ids_ref[i:i + 1, :] for i in range(ROWS_HERE // 128)], axis=1) + 1
    number = lax.broadcasted_iota(I32, (N_ROW, ROWS_HERE), 0)
    mine = all_owners == number * N_COL
    pieces = [jnp.where(mine, part.astype(F32), 0.0).astype(BF16) for part in (values >> 16, (values >> 8) & 255, values & 255)]
    sums = lax.dot_general(
        jnp.concatenate(pieces, axis=0), at_place, (((1,), (1,)), ((), ())), preferred_element_type=F32
    )
    found = (sums[:N_ROW] * 65536.0 + sums[N_ROW:2 * N_ROW] * 256.0 + sums[2 * N_ROW:]).astype(I32)
    for step in range(N_ROW):
        ids_send[step] = found[step:step + 1, :]

    ids_self = pltpu.make_async_copy(ids_send.at[0], ids_recv.at[row], ids_self_sem)
    ids_self.start()

    for group in range(1, N_ROW):
        pltpu.make_async_remote_copy(
            src_ref=ids_send.at[group],
            dst_ref=ids_recv.at[row],
            send_sem=ids_send_sem,
            recv_sem=ids_recv_sem,
            device_id=partner(group, 0),
            device_id_type=MESH,
        ).start()

    pack(3)
    start(3 * BATCH, DEVICES - 1)
    self_copy = pltpu.make_async_copy(send.at[DEVICES - 1], recv.at[col, pl.ds(row * CHUNK, CHUNK)], self_sem)
    self_copy.start()

    table[...] = parity_signs(SLICE)

    def arrived(group):
        chunks = pl.ds(0, N_COL if group else N_COL - 1)
        pltpu.make_async_copy(send.at[chunks], send.at[chunks], recv_sem.at[group]).wait()
        if group == 0:
            self_copy.wait()

    for group in range(N_ROW):
        arrived(group)

    ids_self.wait()
    others = pl.ds(0, N_ROW - 1)
    pltpu.make_async_copy(ids_send.at[others], ids_send.at[others], ids_recv_sem).wait()
    everyone = pl.ds(0, DEVICES - 1)
    pltpu.make_async_copy(send.at[everyone], send.at[everyone], send_sem).wait()
    pltpu.make_async_copy(ids_send.at[others], ids_send.at[others], ids_send_sem).wait()


def finish(recv, table, ids_recv, published, scale_out, ids_out, codes, scale_ref, oid_ref, sem):
    copies = []
    peaks = []
    following = mix(recv, table, 0)
    for first in range(0, SLOTS, SLAB):
        inner = following
        if first + SLAB < SLOTS:
            following = mix(recv, table, first + SLAB)
        peaks += rotate(inner, codes, first)
        part = pl.ds(first, SLAB)
        copies.append(pltpu.make_async_copy(codes.at[part], published.at[part], sem.at[2 + first // SLAB]))
        copies[-1].start()
    for q in range(SLOTS // 128):
        oid_ref[q:q + 1, :] = ids_recv[4 * q] + ids_recv[4 * q + 1] + ids_recv[4 * q + 2] + ids_recv[4 * q + 3] - 1
    copies.append(pltpu.make_async_copy(oid_ref, ids_out, sem.at[0]))
    copies[-1].start()
    diagonal = lax.broadcasted_iota(I32, (128, 128), 0) == lax.broadcasted_iota(I32, (128, 128), 1)
    group = 128 // CHUNK
    scale_ref[...] = jnp.concatenate([
        jnp.sum(jnp.where(diagonal, jnp.concatenate(peaks[q * group:(q + 1) * group], axis=0), 0.0), axis=0, keepdims=True)
        for q in range(SLOTS // 128)
    ], axis=0).astype(BF16)
    copies.append(pltpu.make_async_copy(scale_ref, scale_out, sem.at[1]))
    copies[-1].start()
    for copy in copies:
        copy.wait()


def shards(new_rows, old_rows, row_ids, owner):
    vmem = pl.BlockSpec(memory_space=pltpu.VMEM)
    anywhere = pl.BlockSpec(memory_space=pl.ANY)
    places = np.array([PLACE[(number // N_COL, number % N_COL)] * 2 * CAP for number in range(DEVICES)], np.float32)
    places = jnp.asarray(np.repeat(places[:, None], 128, axis=1))
    received = pl.pallas_call(
        kernel,
        out_shape=(
            jax.ShapeDtypeStruct((N_COL, SLOTS, SLICE), BF16),
            jax.ShapeDtypeStruct((SLICE, SLICE), BF16),
            jax.ShapeDtypeStruct((N_ROW, 1, 128), I32),
        ),
        in_specs=[anywhere] * 5,
        out_specs=(vmem,) * 3,
        scratch_shapes=[
            pltpu.VMEM((ROWS_HERE, SLICE), F32),
            pltpu.VMEM((ROWS_HERE, SLICE), F32),
            pltpu.VMEM((ROWS_HERE // 128, 128), I32),
            pltpu.VMEM((ROWS_HERE // 128, 128), I32),
            pltpu.VMEM((DEVICES, 128), F32),
            pltpu.VMEM((ROWS_HERE, SLICE), BF16),
            pltpu.VMEM((DEVICES, CHUNK, SLICE), BF16),
            pltpu.VMEM((N_ROW, 1, 128), I32),
            pltpu.SemaphoreType.DMA((2 * PAIRS,)),
            pltpu.SemaphoreType.DMA((3,)),
            pltpu.SemaphoreType.REGULAR,
            pltpu.SemaphoreType.REGULAR,
            pltpu.SemaphoreType.REGULAR,
            pltpu.SemaphoreType.DMA,
            pltpu.SemaphoreType.DMA((N_ROW,)),
            pltpu.SemaphoreType.DMA,
            pltpu.SemaphoreType.DMA,
            pltpu.SemaphoreType.DMA,
            pltpu.SemaphoreType.DMA,
        ],
        compiler_params=pltpu.CompilerParams(
            collective_id=0, has_side_effects=True, vmem_limit_bytes=40 * 1024 * 1024
        ),
    )(*(
        pltpu.with_memory_space_constraint(array, pltpu.HBM)
        for array in (new_rows, old_rows, owner.reshape(ROWS_HERE // 128, 128), row_ids.reshape(ROWS_HERE // 128, 128), places)
    ))
    published, scale, ids = pl.pallas_call(
        finish,
        out_shape=(
            jax.ShapeDtypeStruct((SLOTS, D), BF16),
            jax.ShapeDtypeStruct((SLOTS // 128, 128), BF16),
            jax.ShapeDtypeStruct((SLOTS // 128, 128), I32),
        ),
        in_specs=[vmem] * 3,
        out_specs=(anywhere,) * 3,
        scratch_shapes=[
            pltpu.VMEM((SLOTS, D), BF16),
            pltpu.VMEM((SLOTS // 128, 128), BF16),
            pltpu.VMEM((SLOTS // 128, 128), I32),
            pltpu.SemaphoreType.DMA((2 + SLOTS // SLAB,)),
        ],
        compiler_params=pltpu.CompilerParams(vmem_limit_bytes=8 * 1024 * 1024),
    )(*(pltpu.with_memory_space_constraint(array, pltpu.VMEM) for array in received))
    return published, scale.reshape(SLOTS), ids.reshape(SLOTS)


def solution(mesh):
    return jax.shard_map(
        shards,
        mesh=mesh,
        in_specs=(P("row", "col"), P("row", "col"), P("row"), P("row", None)),
        out_specs=(P(("row", "col"), None), P(("row", "col")), P(("row", "col"))),
        check_vma=False,
    )
```
